32 devices in a mesh: seq: 16 (over z, y, x), fsdp: 2 (over core).
Axes of the slice: x: 2, y: 2, z: 4, core: 2. Of those that a mesh axis runs over, the one named last changes fastest.
Arguments:
- query: bfloat16 [8192, 4096], P('seq', 'fsdp'), may hold values from -6 to 6
- key: bfloat16 [8192, 4096], P('seq', 'fsdp'), may hold values from -6 to 6
- value: bfloat16 [8192, 4096], P('seq', 'fsdp'), may hold values from -16 to 16, as said below
- cotangent: bfloat16 [8192, 4096], P('seq', 'fsdp'), may hold values from -6 to 6
- gain: float32 [4096], P('fsdp'), may hold values from 0.1 to 1.9
Outputs:
- query_grad: bfloat16 [8192, 4096], P('seq', 'fsdp')
- key_grad: bfloat16 [8192, 4096], P('seq', 'fsdp')
- value_grad: bfloat16 [8192, 4096], P('seq', 'fsdp')
- gain_grad: float32 [4096], P('fsdp')
The draws below stay inside these ranges and needn't reach their ends.
Inputs may be any that keep to these rules, and one draw needn't show every extreme that they name: `value`: values whose typical size differs from head to head.
All inputs are finite; a program needn't handle non-finite values.
Results may differ from the reference program's by a relative error of at most 0.0057.
Values sent between devices are 32-bit elements; how exact they have to be, the bound alone decides.
A program may use at most 128 MiB of HBM per device.

```python
import math
import jax
import jax.numpy as jnp
from jax import lax

HEADS = 32
HEAD_DIM = 128
TOK_DEV = 512
HD = 4096
LENGTH = 8192


def draw_value(key, part):
    head = (jnp.arange(HD) // HEAD_DIM).astype(jnp.float32)
    rising = jnp.exp(math.log(3.0) * head / max(HEADS - 1, 1))
    noise = jnp.clip(jax.random.normal(jax.random.fold_in(key, 1), (LENGTH, HD), jnp.float32), -4.0, 4.0)
    return (noise * rising[None, :]).astype(jnp.bfloat16)


def spiked(result, rng, source, target, blocks, factor):
    def block_of(position):
        return (jnp.arange(result.shape[position]) // (result.shape[position] // blocks)).reshape((-1,) + (1,) * (result.ndim - 1 - position))

    near = jax.random.permutation(rng, blocks)[block_of(target)]
    second = (block_of(target) + blocks // 2) % blocks
    return jnp.where((block_of(source) == near) | (block_of(source) == second), factor * result, result)


def level_of(own_key, dims, pieces, low, top_value):
    factor_of, own = 1.0, jax.random.fold_in(own_key, 6)
    for dim, blocks in pieces:
        draws = jnp.exp(jax.random.uniform(jax.random.fold_in(own, dim), (blocks,), jnp.float32, low / len(pieces), top_value / len(pieces)))
        factor_of = factor_of * jnp.repeat(draws, dims[dim] // blocks).reshape([-1 if axis == dim else 1 for axis in range(len(dims))])
    return factor_of


def normal_values(key, extent, spread, most, shards=(), kind=jnp.bfloat16):
    result = jax.random.normal(key, extent, jnp.float32) * spread
    if len(shards) > 0:
        result = level_of(key, extent, shards, -0.22, 0.18) * result
    return jnp.clip(result, min=-most, max=most).astype(kind)


def bell_draw_with(key, shape, deviation, limit, pieces, heavy, kind=jnp.bfloat16):
    array = deviation * jax.random.normal(key, shape, jnp.float32)
    if pieces:
        array = array * level_of(key, shape, pieces, -0.22, 0.18)
    return jnp.clip(spiked(array, jax.random.fold_in(key, 3), *heavy), -limit, limit).astype(kind)


def setup_inputs(seed: int = 0) -> dict:
    key_of = jax.random.split(jax.random.key(seed), 6)
    query = normal_values(key_of[0], (LENGTH, HD), 1.0, 6.0, ((0, 16), (1, 2)))
    key = normal_values(key_of[1], (LENGTH, HD), 1.0, 6.0, ((0, 16), (1, 2)))
    value = draw_value(jax.random.fold_in(key_of[5], 71), 0)
    cotangent = bell_draw_with(key_of[3], (LENGTH, HD), 1.0, 6.0, ((0, 16), (1, 2)), (0, 1, 16, 2.0))
    gain = jnp.clip(1.0 + 0.18 * jax.random.normal(key_of[4], (HD,), jnp.float32), 0.1, 1.9)
    return {"query": query, "key": key, "value": value, "cotangent": cotangent, "gain": gain}


def block_state(items):
    left = items[0].astype(jnp.float32)
    right = items[1].astype(jnp.float32)
    return jnp.einsum('tha,thb->hab', left, right)

def reference(query, key, value, cotangent, gain):
    blocks = LENGTH // TOK_DEV
    shape = (blocks, TOK_DEV, HEADS, HEAD_DIM)
    qb = query.reshape(shape)
    kb = key.reshape(shape)
    vb = value.reshape(shape)
    causal = jnp.tril(jnp.ones((TOK_DEV, TOK_DEV), dtype=bool))
    states = lax.map(block_state, (kb, vb))
    zeros = jnp.zeros_like(states[:1])
    prefix = jnp.concatenate([zeros, jnp.cumsum(states, axis=0)[:-1]], axis=0)
    prefix_low = prefix.astype(jnp.bfloat16).astype(jnp.float32)

    def forward(items):
        qf = items[0].astype(jnp.float32)
        kf = items[1].astype(jnp.float32)
        vf = items[2].astype(jnp.float32)
        scores = jnp.einsum('tha,sha->hts', qf, kf)
        weights = jnp.where(causal[None], scores, 0.0).astype(jnp.bfloat16).astype(jnp.float32)
        out = jnp.einsum('hts,shb->thb', weights, vf) + jnp.einsum('tha,hab->thb', qf, items[3])
        return out.reshape(TOK_DEV, HD)
    attended = lax.map(forward, (qb, kb, vb, prefix_low)).reshape(LENGTH, HD)
    inv_rms = lax.rsqrt(lax.optimization_barrier(jnp.mean(attended * attended, axis=-1, keepdims=True)) + 1e-05)
    normed = attended * inv_rms
    upstream = cotangent.astype(jnp.float32)
    gain_grad = lax.optimization_barrier(jnp.sum(upstream * normed, axis=0)) * (1.0 / math.sqrt(LENGTH))
    scaled = upstream * gain
    attended_grad = (scaled - normed * lax.optimization_barrier(jnp.mean(scaled * normed, axis=-1, keepdims=True))) * inv_rms
    dof = attended_grad.astype(jnp.bfloat16).astype(jnp.float32).reshape(shape)
    grad_states = lax.map(block_state, (qb, dof))
    suffix = jnp.concatenate([jnp.cumsum(grad_states[::-1], axis=0)[::-1][1:], zeros], axis=0)
    suffix_low = suffix.astype(jnp.bfloat16).astype(jnp.float32)

    def backward(items):
        qf = items[0].astype(jnp.float32)
        kf = items[1].astype(jnp.float32)
        vf = items[2].astype(jnp.float32)
        grads = items[3]
        pre = items[4]
        suf = items[5]
        scores = jnp.einsum('tha,sha->hts', qf, kf)
        weights = jnp.where(causal[None], scores, 0.0).astype(jnp.bfloat16).astype(jnp.float32)
        score_grad = jnp.einsum('thb,shb->hts', grads, vf)
        score_grad = jnp.where(causal[None], score_grad, 0.0).astype(jnp.bfloat16).astype(jnp.float32)
        q_grad = jnp.einsum('hts,sha->tha', score_grad, kf) + jnp.einsum('thb,hab->tha', grads, pre)
        k_grad = jnp.einsum('hts,tha->sha', score_grad, qf) + jnp.einsum('shb,hab->sha', vf, suf)
        v_grad = jnp.einsum('hts,thb->shb', weights, grads) + jnp.einsum('sha,hab->shb', kf, suf)
        flat = (TOK_DEV, HD)
        return (q_grad.reshape(flat).astype(jnp.bfloat16), k_grad.reshape(flat).astype(jnp.bfloat16), v_grad.reshape(flat).astype(jnp.bfloat16))
    query_grad, key_grad, value_grad = lax.map(backward, (qb, kb, vb, dof, prefix_low, suffix_low))
    flat = (LENGTH, HD)
    return (query_grad.reshape(flat), key_grad.reshape(flat), value_grad.reshape(flat), gain_grad)
```

```python
import functools
import math

import jax
import jax.numpy as jnp
from jax import lax
from jax.experimental import pallas as pl
from jax.experimental.pallas import tpu as pltpu
from jax.sharding import PartitionSpec as P

HEAD_DIM = 128
HD = 4096
EPS = 1e-05
MESH = pl.DeviceIdType.MESH
F32 = jnp.float32
BF16 = jnp.bfloat16


def dot_ab(a, b):
    return lax.dot_general(a, b, (((1,), (0,)), ((), ())), preferred_element_type=F32)


def dot_abt(a, b):
    return lax.dot_general(a, b, (((1,), (1,)), ((), ())), preferred_element_type=F32)


def dot_atb(a, b):
    return lax.dot_general(a, b, (((0,), (0,)), ((), ())), preferred_element_type=F32)


def group_size(count):
    size = 1
    while size * size < count:
        size *= 2
    return size


def lower(block, offset):
    row = lax.broadcasted_iota(jnp.int32, block.shape, 0) + offset
    col = lax.broadcasted_iota(jnp.int32, block.shape, 1)
    return jnp.where(row >= col, block, 0.0).astype(BF16)


def upper(block):
    row = lax.broadcasted_iota(jnp.int32, block.shape, 0)
    col = lax.broadcasted_iota(jnp.int32, block.shape, 1)
    return jnp.where(row <= col, block, 0.0).astype(BF16)


def cols_of(head):
    return pl.ds(pl.multiple_of(head * HEAD_DIM, HEAD_DIM), HEAD_DIM)


class Scan:
    def __init__(self, which, reverse, g, m, chunks, refs, sems):
        self.which, self.reverse, self.g, self.m, self.chunks = which, reverse, g, m, chunks
        self.own, self.slots, self.carry, self.fwd, self.outs, self.result = refs
        self.a_send, self.a_recv, self.z_send, self.z_recv, self.b_send, self.b_recv = sems
        me = lax.axis_index("seq")
        self.z, self.i = me // g, lax.rem(me, g)
        self.piece = self.own.shape[0] // g
        self.ch = self.piece // chunks

    def peer(self, d):
        return lax.rem(self.i + d, self.g)

    def rows(self, p, j):
        return pl.ds(pl.multiple_of(p * self.piece + j * self.ch, self.ch), self.ch)

    def part(self, j):
        return pl.ds(j * self.ch, self.ch)

    def spread(self, d, j, arriving=False):
        p = self.peer(d)
        slot = p if arriving else self.i
        return pltpu.make_async_remote_copy(
            src_ref=self.own.at[self.rows(p, j)],
            dst_ref=self.slots.at[slot, self.part(j)],
            send_sem=self.a_send.at[self.which, d, j],
            recv_sem=self.a_recv.at[self.which, slot, j],
            device_id={"seq": self.z * self.g + p},
            device_id_type=MESH,
        )

    def chain(self, j):
        nearer = self.z - 1 if self.reverse else self.z + 1
        target = jnp.clip(nearer, 0, self.m - 1)
        return pltpu.make_async_remote_copy(
            src_ref=self.fwd.at[self.part(j)],
            dst_ref=self.carry.at[self.part(j)],
            send_sem=self.z_send.at[self.which, j],
            recv_sem=self.z_recv.at[self.which, j],
            device_id={"seq": target * self.g + self.i},
            device_id_type=MESH,
        )

    def hand(self, d, j, arriving=False):
        p = self.peer(d)
        owner = p if arriving else self.i
        return pltpu.make_async_remote_copy(
            src_ref=self.outs.at[p, self.part(j)],
            dst_ref=self.result.at[self.rows(owner, j)],
            send_sem=self.b_send.at[self.which, d, j],
            recv_sem=self.b_recv.at[self.which, owner, j],
            device_id={"seq": self.z * self.g + p},
            device_id_type=MESH,
        )

    def first(self):
        return self.z == (self.m - 1 if self.reverse else 0)

    def last(self):
        return self.z == (0 if self.reverse else self.m - 1)

    def process(self, j):
        part = self.part(j)
        for d in range(1, self.g):
            self.spread(d, j, True).wait_recv()
        total = self.slots[0, part]
        for p in range(1, self.g):
            total = total + self.slots[p, part]

        @pl.when(self.first())
        def _():
            self.carry[part] = jnp.zeros_like(total)

        @pl.when(jnp.logical_not(self.first()))
        def _():
            self.chain(j).wait_recv()

        @pl.when(jnp.logical_not(self.last()))
        def _():
            self.fwd[part] = self.carry[part] + total
            self.chain(j).start()

        running = self.carry[part]
        order = range(self.g)
        for p in reversed(order) if self.reverse else order:
            self.outs[p, part] = running
            running = running + self.slots[p, part]
        for d in range(1, self.g):
            self.hand(d, j).start()
        self.result[self.rows(self.i, j)] = self.outs[self.i, part]

    def drain(self):
        for j in range(self.chunks):
            for d in range(1, self.g):
                self.spread(d, j).wait_send()
                self.hand(d, j).wait_send()

            @pl.when(jnp.logical_not(self.last()))
            def _():
                self.chain(j).wait_send()


def kernel(
    n, g, fs, chunks, groups,
    q_hbm, k_hbm, v_hbm, c_hbm, gain_ref,
    qg_hbm, kg_hbm, vg_hbm, gg_ref,
    q, k, v, cot, do, att, kg_l, vg_l, qg, kg, vg,
    own, slots, carry, fwd, outs, result,
    sq, cr, stats, gp, gz,
    in_sem, out_sem, a_send, a_recv, z_send, z_recv, b_send, b_recv,
    f_send, f_recv, g_send, g_recv, h_send, h_recv,
):
    rows, width = q.shape
    heads = width // HEAD_DIM
    half = rows // 2
    m = n // g
    me = lax.axis_index("seq")
    mine = lax.axis_index("fsdp")
    z, i = me // g, lax.rem(me, g)

    loads = [
        pltpu.make_async_copy(src, dst, in_sem.at[at])
        for at, (src, dst) in enumerate(((k_hbm, k), (v_hbm, v), (q_hbm, q), (c_hbm, cot)))
    ]
    for load in loads:
        load.start()

    barrier = pltpu.get_barrier_semaphore()
    for d in range(1, g):
        pl.semaphore_signal(
            barrier, inc=1, device_id={"seq": z * g + lax.rem(i + d, g)}, device_id_type=MESH
        )
    for d in range(1, m):
        pl.semaphore_signal(
            barrier, inc=1, device_id={"seq": lax.rem(z + d, m) * g + i}, device_id_type=MESH
        )
    for d in range(1, fs):
        pl.semaphore_signal(
            barrier, inc=1, device_id={"fsdp": lax.rem(mine + d, fs)}, device_id_type=MESH
        )

    sems = (a_send, a_recv, z_send, z_recv, b_send, b_recv)
    scans = [
        Scan(w, w == 1, g, m, chunks, tuple(r.at[w] for r in (own, slots, carry, fwd, outs, result)), sems)
        for w in range(2)
    ]
    per = heads // g

    def head_order(turn):
        if per:
            for j in range(chunks):
                for d in range(g):
                    turn(lax.rem(i + d, g) * per + j, d, j)

    def make_states(scan, state_of):
        def turn(head, d, j):
            state = state_of(head)
            if d == 0:
                scan.slots[i, scan.part(j)] = state
            else:
                scan.own[scan.rows(scan.peer(d), j)] = state
                scan.spread(d, j).start()

        if per:
            for j in range(chunks):
                for d in list(range(1, g)) + [0]:
                    turn(lax.rem(i + d, g) * per + j, d, j)
        else:
            for head in range(heads):
                scan.own[pl.ds(head * HEAD_DIM, HEAD_DIM)] = state_of(head)
            for j in range(chunks):
                scan.slots[i, scan.part(j)] = scan.own[scan.rows(i, j)]
                for d in range(1, g):
                    scan.spread(d, j).start()

    def arrivals(scan, visit):
        if per:
            for j in range(chunks):
                for d in range(g):
                    if d:
                        scan.hand(d, j, True).wait_recv()
                    visit(lax.rem(i + d, g) * per + j)
        else:
            for j in range(chunks):
                for d in range(1, g):
                    scan.hand(d, j, True).wait_recv()
            for head in range(heads):
                visit(head)

    def state_at(scan, head):
        at = pl.ds(pl.multiple_of(head * HEAD_DIM, HEAD_DIM), HEAD_DIM)
        return scan.result[at].astype(BF16)

    loads[0].wait()
    loads[1].wait()
    pl.semaphore_wait(barrier, (g - 1) + (m - 1) + (fs - 1))
    make_states(scans[0], lambda head: dot_atb(k[:, cols_of(head)], v[:, cols_of(head)]))
    loads[2].wait()

    top, low = pl.ds(0, half), pl.ds(half, half)

    def inside(head, _):
        cols = cols_of(head)
        kh, vh = k[:, cols], v[:, cols]
        w0 = lower(dot_abt(q[top, cols], k[top, cols]), 0)
        w1 = lower(dot_abt(q[low, cols], kh), half)
        att[top, cols] = dot_ab(w0, v[top, cols])
        att[low, cols] = dot_ab(w1, vh)
        return 0

    for j in range(chunks):
        lax.fori_loop(groups[j], groups[j + 1], inside, 0)
        scans[0].process(j)
    lax.fori_loop(groups[chunks], heads, inside, 0)
    loads[3].wait()

    sq[...] = jnp.zeros_like(sq)
    cr[...] = jnp.zeros_like(cr)

    def finish(head):
        cols = cols_of(head)
        a = att[:, cols] + dot_ab(q[:, cols], state_at(scans[0], head))
        att[:, cols] = a
        sq[...] += a * a
        cr[...] += a * (cot[:, cols].astype(F32) * gain_ref[:, cols])

    arrivals(scans[0], finish)

    lane = lax.broadcasted_iota(jnp.int32, sq.shape, 1)
    stats[mine] = jnp.where(
        lane < HEAD_DIM // 2,
        jnp.sum(sq[...], axis=1, keepdims=True),
        jnp.sum(cr[...], axis=1, keepdims=True),
    )

    def share(d, slot):
        return pltpu.make_async_remote_copy(
            src_ref=stats.at[mine],
            dst_ref=stats.at[slot],
            send_sem=f_send.at[d],
            recv_sem=f_recv.at[slot],
            device_id={"fsdp": lax.rem(mine + d, fs)},
            device_id_type=MESH,
        )

    for d in range(1, fs):
        share(d, mine).start()
    for d in range(1, fs):
        share(d, lax.rem(mine + d, fs)).wait_recv()
    both = stats[0]
    for f in range(1, fs):
        both = both + stats[f]
    inv = lax.rsqrt(both[:, 0:1] / HD + EPS)
    mean = both[:, HEAD_DIM - 1 : HEAD_DIM] * inv / HD
    sq[...] = jnp.broadcast_to(inv, sq.shape)
    cr[...] = jnp.broadcast_to(mean, cr.shape)

    def grad_state(head):
        cols = cols_of(head)
        up = cot[:, cols].astype(F32)
        normed = att[:, cols] * sq[...]
        gp[i, :, cols] = jnp.sum(up * normed, axis=0, keepdims=True)
        d_h = ((up * gain_ref[:, cols] - normed * cr[...]) * sq[...]).astype(BF16)
        do[:, cols] = d_h
        return dot_atb(q[:, cols], d_h)

    make_states(scans[1], grad_state)

    def gain_near(d, slot):
        return pltpu.make_async_remote_copy(
            src_ref=gp.at[i],
            dst_ref=gp.at[slot],
            send_sem=g_send.at[d],
            recv_sem=g_recv.at[slot],
            device_id={"seq": z * g + lax.rem(i + d, g)},
            device_id_type=MESH,
        )

    def gain_far(d, slot):
        return pltpu.make_async_remote_copy(
            src_ref=gz.at[z],
            dst_ref=gz.at[slot],
            send_sem=h_send.at[d],
            recv_sem=h_recv.at[slot],
            device_id={"seq": lax.rem(z + d, m) * g + i},
            device_id_type=MESH,
        )

    for d in range(1, g):
        gain_near(d, i).start()

    def backward(head, _):
        cols = cols_of(head)
        qh, kh, vh, dh = q[:, cols], k[:, cols], v[:, cols], do[:, cols]
        q1, k0, v0, d1 = q[low, cols], k[top, cols], v[top, cols], do[low, cols]
        from_prefix = dot_abt(dh, state_at(scans[0], head))
        s0 = lower(dot_abt(do[top, cols], v0), 0)
        s1 = lower(dot_abt(d1, vh), half)
        qg[top, cols] = (dot_ab(s0, k0) + from_prefix[:half]).astype(BF16)
        qg[low, cols] = (dot_ab(s1, kh) + from_prefix[half:]).astype(BF16)
        t0 = upper(dot_abt(v0, dh))
        t1 = upper(dot_abt(v[low, cols], d1))
        kg_l[top, cols] = dot_ab(t0, qh)
        kg_l[low, cols] = dot_ab(t1, q1)
        w0 = upper(dot_abt(k0, qh))
        w1 = upper(dot_abt(k[low, cols], q1))
        vg_l[top, cols] = dot_ab(w0, dh)
        vg_l[low, cols] = dot_ab(w1, d1)
        return 0

    for j in range(chunks):
        lax.fori_loop(groups[j], groups[j + 1], backward, 0)
        scans[1].process(j)
    lax.fori_loop(groups[chunks], heads, backward, 0)
    store_q = pltpu.make_async_copy(qg, qg_hbm, out_sem.at[0, 0])
    store_q.start()

    for d in range(1, g):
        gain_near(d, lax.rem(i + d, g)).wait_recv()
    near = gp[0]
    for p in range(1, g):
        near = near + gp[p]
    gz[z] = near
    for d in range(1, m):
        gain_far(d, z).start()

    def store(at, src, dst, head):
        cols = cols_of(head)
        return pltpu.make_async_copy(src.at[:, cols], dst.at[:, cols], out_sem.at[at, head])

    def last(head):
        cols = cols_of(head)
        suffix = state_at(scans[1], head)
        kg[:, cols] = (kg_l[:, cols] + dot_abt(v[:, cols], suffix)).astype(BF16)
        vg[:, cols] = (vg_l[:, cols] + dot_ab(k[:, cols], suffix)).astype(BF16)
        store(1, kg, kg_hbm, head).start()
        store(2, vg, vg_hbm, head).start()

    arrivals(scans[1], last)

    for d in range(1, m):
        gain_far(d, lax.rem(z + d, m)).wait_recv()
    total = gz[0]
    for p in range(1, m):
        total = total + gz[p]
    gg_ref[...] = total * (1.0 / math.sqrt(rows * n))

    for scan in scans:
        scan.drain()
    for d in range(1, fs):
        share(d, mine).wait_send()
    for d in range(1, g):
        gain_near(d, i).wait_send()
    for d in range(1, m):
        gain_far(d, z).wait_send()
    store_q.wait()

    def stored(head, _):
        store(1, kg, kg_hbm, head).wait()
        store(2, vg, vg_hbm, head).wait()
        return 0

    lax.fori_loop(0, heads, stored, 0)


def solution(mesh):
    n, fs = mesh.shape["seq"], mesh.shape["fsdp"]
    g = group_size(n)
    m = n // g

    def shards(query, key, value, cotangent, gain):
        rows, width = query.shape
        heads = width // HEAD_DIM
        chunks = max(heads // g, 1)
        state = heads * HEAD_DIM
        piece = state // g
        step = heads // (chunks + 1)
        groups = tuple(min(heads, (j * heads) // (chunks + 1)) for j in range(chunks + 1))
        any_space = pl.BlockSpec(memory_space=pl.ANY)
        vmem = pl.BlockSpec(memory_space=pltpu.VMEM)
        dma = pltpu.SemaphoreType.DMA
        big, small = jax.ShapeDtypeStruct((rows, width), BF16), jax.ShapeDtypeStruct((1, width), F32)
        products = 6 * rows * rows + 6 * rows * HEAD_DIM
        results = pl.pallas_call(
            functools.partial(kernel, n, g, fs, chunks, groups),
            out_shape=(big, big, big, small),
            in_specs=[any_space] * 4 + [vmem],
            out_specs=(any_space, any_space, any_space, vmem),
            scratch_shapes=[pltpu.VMEM((rows, width), BF16)] * 5
            + [pltpu.VMEM((rows, width), F32)] * 3
            + [pltpu.VMEM((rows, width), BF16)] * 3
            + [
                pltpu.VMEM((2, state, HEAD_DIM), F32),
                pltpu.VMEM((2, g, piece, HEAD_DIM), F32),
                pltpu.VMEM((2, piece, HEAD_DIM), F32),
                pltpu.VMEM((2, piece, HEAD_DIM), F32),
                pltpu.VMEM((2, g, piece, HEAD_DIM), F32),
                pltpu.VMEM((2, state, HEAD_DIM), F32),
                pltpu.VMEM((rows, HEAD_DIM), F32),
                pltpu.VMEM((rows, HEAD_DIM), F32),
                pltpu.VMEM((fs, rows, HEAD_DIM), F32),
                pltpu.VMEM((g, 1, width), F32),
                pltpu.VMEM((m, 1, width), F32),
                dma((4,)),
                dma((3, heads)),
                dma((2, g, chunks)),
                dma((2, g, chunks)),
                dma((2, chunks)),
                dma((2, chunks)),
                dma((2, g, chunks)),
                dma((2, g, chunks)),
                dma((fs,)),
                dma((fs,)),
                dma((g,)),
                dma((g,)),
                dma((m,)),
                dma((m,)),
            ],
            compiler_params=pltpu.CompilerParams(
                collective_id=0, has_side_effects=True, vmem_limit_bytes=56 * 2**20
            ),
            cost_estimate=pl.CostEstimate(
                flops=2 * products * width, bytes_accessed=14 * rows * width, transcendentals=rows
            ),
        )(query, key, value, cotangent, gain.reshape(1, width))
        return results[0], results[1], results[2], results[3].reshape(width)

    in_specs = (P("seq", "fsdp"), P("seq", "fsdp"), P("seq", "fsdp"), P("seq", "fsdp"), P("fsdp"))
    out_specs = (P("seq", "fsdp"), P("seq", "fsdp"), P("seq", "fsdp"), P("fsdp"))
    return jax.shard_map(shards, mesh=mesh, in_specs=in_specs, out_specs=out_specs, check_vma=False)
```

```python
import functools
import math

import jax
import jax.numpy as jnp
from jax import lax
from jax.experimental import pallas as pl
from jax.experimental.pallas import tpu as pltpu
from jax.sharding import PartitionSpec as P

HEAD_DIM = 128
HD = 4096
EPS = 1e-05
MESH = pl.DeviceIdType.MESH
F32 = jnp.float32
BF16 = jnp.bfloat16


def dot_ab(a, b):
    return lax.dot_general(a, b, (((1,), (0,)), ((), ())), preferred_element_type=F32)


def dot_abt(a, b):
    return lax.dot_general(a, b, (((1,), (1,)), ((), ())), preferred_element_type=F32)


def dot_atb(a, b):
    return lax.dot_general(a, b, (((0,), (0,)), ((), ())), preferred_element_type=F32)


def group_size(count):
    size = 1
    while size * size < count:
        size *= 2
    return size


def lower(block, offset):
    row = lax.broadcasted_iota(jnp.int32, block.shape, 0) + offset
    col = lax.broadcasted_iota(jnp.int32, block.shape, 1)
    return jnp.where(row >= col, block, 0.0).astype(BF16)


def upper(block):
    row = lax.broadcasted_iota(jnp.int32, block.shape, 0)
    col = lax.broadcasted_iota(jnp.int32, block.shape, 1)
    return jnp.where(row <= col, block, 0.0).astype(BF16)


def cols_of(head):
    return pl.ds(pl.multiple_of(head * HEAD_DIM, HEAD_DIM), HEAD_DIM)


class Scan:
    def __init__(self, which, reverse, g, m, chunks, refs, sems):
        self.which, self.reverse, self.g, self.m, self.chunks = which, reverse, g, m, chunks
        self.own, self.slots, self.carry, self.fwd, self.before, self.outs, self.result = refs
        self.a_send, self.a_recv, self.z_send, self.z_recv, self.b_send, self.b_recv = sems
        me = lax.axis_index("seq")
        self.z, self.i = me // g, lax.rem(me, g)
        self.piece = self.own.shape[0] // g
        self.ch = self.piece // chunks

    def peer(self, d):
        return lax.rem(self.i + d, self.g)

    def rows(self, p, j):
        return pl.ds(pl.multiple_of(p * self.piece + j * self.ch, self.ch), self.ch)

    def part(self, j):
        return pl.ds(j * self.ch, self.ch)

    def spread(self, d, j, arriving=False):
        p = self.peer(d)
        slot = p if arriving else self.i
        return pltpu.make_async_remote_copy(
            src_ref=self.own.at[self.rows(p, j)],
            dst_ref=self.slots.at[slot, self.part(j)],
            send_sem=self.a_send.at[self.which, d, j],
            recv_sem=self.a_recv.at[self.which, slot, j],
            device_id={"seq": self.z * self.g + p},
            device_id_type=MESH,
        )

    def place(self):
        return self.m - 1 - self.z if self.reverse else self.z

    def chain(self, level, t, j):
        place = jnp.clip(self.place() + 1 + t, 0, self.m - 1)
        group = self.m - 1 - place if self.reverse else place
        return pltpu.make_async_remote_copy(
            src_ref=self.fwd.at[level, self.part(j)],
            dst_ref=self.carry.at[level, self.part(j)],
            send_sem=self.z_send.at[self.which, level, t, j],
            recv_sem=self.z_recv.at[self.which, level, j],
            device_id={"seq": group * self.g + self.i},
            device_id_type=MESH,
        )

    def levels(self):
        return range(self.m.bit_length() - 1)

    def sends(self, level):
        return lax.rem(self.place(), 2 << level) == (1 << level) - 1

    def receives(self, level):
        return lax.rem(self.place(), 2 << level) >= 1 << level

    def forward(self, level, j, value):
        @pl.when(self.sends(level))
        def _():
            self.fwd[level, self.part(j)] = value()
            for t in range(1 << level):
                self.chain(level, t, j).start()

    def hand(self, d, j, arriving=False):
        p = self.peer(d)
        owner = p if arriving else self.i
        return pltpu.make_async_remote_copy(
            src_ref=self.outs.at[p, self.part(j)],
            dst_ref=self.result.at[self.rows(owner, j)],
            send_sem=self.b_send.at[self.which, d, j],
            recv_sem=self.b_recv.at[self.which, owner, j],
            device_id={"seq": self.z * self.g + p},
            device_id_type=MESH,
        )

    def total(self, j):
        total = self.slots[0, self.part(j)]
        for p in range(1, self.g):
            total = total + self.slots[p, self.part(j)]
        return total

    def gather(self, j):
        for d in range(1, self.g):
            self.spread(d, j, True).wait_recv()
        if self.m > 1:
            self.forward(0, j, lambda: self.total(j))

    def process(self, j):
        part = self.part(j)
        self.before[part] = jnp.zeros((self.ch, HEAD_DIM), F32)
        for level in self.levels():
            if level:
                self.forward(level, j, lambda: self.before[part] + self.total(j))

            @pl.when(self.receives(level))
            def _():
                self.chain(level, 0, j).wait_recv()
                self.before[part] += self.carry[level, part]

        running = self.before[part]
        order = range(self.g)
        for p in reversed(order) if self.reverse else order:
            self.outs[p, part] = running
            running = running + self.slots[p, part]
        for d in range(1, self.g):
            self.hand(d, j).start()
        self.result[self.rows(self.i, j)] = self.outs[self.i, part]

    def drain(self):
        for j in range(self.chunks):
            for d in range(1, self.g):
                self.spread(d, j).wait_send()
                self.hand(d, j).wait_send()

            for level in self.levels():

                @pl.when(self.sends(level))
                def _():
                    for t in range(1 << level):
                        self.chain(level, t, j).wait_send()


def kernel(
    n, g, fs, chunks,
    q_hbm, k_hbm, v_hbm, c_hbm, gain_ref,
    qg, kg, vg, gg_ref,
    q, k, v, cot, do, att, kg_l, vg_l, w_top, w_low,
    own, slots, carry, fwd, before, outs, result,
    sq, cr, stats, gp, gz,
    in_sem, a_send, a_recv, z_send, z_recv, b_send, b_recv,
    f_send, f_recv, g_send, g_recv, h_send, h_recv,
):
    rows, width = q.shape
    heads = width // HEAD_DIM
    half = rows // 2
    m = n // g
    me = lax.axis_index("seq")
    mine = lax.axis_index("fsdp")
    z, i = me // g, lax.rem(me, g)

    loads = [
        pltpu.make_async_copy(src, dst, in_sem.at[at])
        for at, (src, dst) in enumerate(((k_hbm, k), (v_hbm, v), (q_hbm, q), (c_hbm, cot)))
    ]
    for load in loads:
        load.start()

    barrier = pltpu.get_barrier_semaphore()
    for d in range(1, g):
        pl.semaphore_signal(
            barrier, inc=1, device_id={"seq": z * g + lax.rem(i + d, g)}, device_id_type=MESH
        )
    for d in range(1, m):
        pl.semaphore_signal(
            barrier, inc=1, device_id={"seq": lax.rem(z + d, m) * g + i}, device_id_type=MESH
        )
    for d in range(1, fs):
        pl.semaphore_signal(
            barrier, inc=1, device_id={"fsdp": lax.rem(mine + d, fs)}, device_id_type=MESH
        )

    sems = (a_send, a_recv, z_send, z_recv, b_send, b_recv)
    scans = [
        Scan(w, w == 1, g, m, chunks, tuple(r.at[w] for r in (own, slots, carry, fwd, before, outs, result)), sems)
        for w in range(2)
    ]
    per = heads // g

    def head_order(turn):
        if per:
            for j in range(chunks):
                for d in range(g):
                    turn(lax.rem(i + d, g) * per + j, d, j)

    def make_states(scan, state_of):
        def turn(head, d, j):
            state = state_of(head)
            if d == 0:
                scan.slots[i, scan.part(j)] = state
            else:
                scan.own[scan.rows(scan.peer(d), j)] = state
                scan.spread(d, j).start()

        if per:
            for j in range(chunks):
                for d in list(range(1, g)) + [0]:
                    turn(lax.rem(i + d, g) * per + j, d, j)
        else:
            for head in range(heads):
                scan.own[pl.ds(head * HEAD_DIM, HEAD_DIM)] = state_of(head)
            for j in range(chunks):
                scan.slots[i, scan.part(j)] = scan.own[scan.rows(i, j)]
                for d in range(1, g):
                    scan.spread(d, j).start()

    def arrivals(scan, visit):
        if per:
            for j in range(chunks):
                for d in range(g):
                    if d:
                        scan.hand(d, j, True).wait_recv()
                    visit(lax.rem(i + d, g) * per + j)
        else:
            for j in range(chunks):
                for d in range(1, g):
                    scan.hand(d, j, True).wait_recv()
            for head in range(heads):
                visit(head)

    def state_at(scan, head):
        at = pl.ds(pl.multiple_of(head * HEAD_DIM, HEAD_DIM), HEAD_DIM)
        return scan.result[at].astype(BF16)

    loads[0].wait()
    loads[1].wait()
    pl.semaphore_wait(barrier, (g - 1) + (m - 1) + (fs - 1))
    make_states(scans[0], lambda head: dot_atb(k[:, cols_of(head)], v[:, cols_of(head)]))
    loads[2].wait()

    top, low = pl.ds(0, half), pl.ds(half, half)

    def inside(head, _):
        cols = cols_of(head)
        kh, vh = k[:, cols], v[:, cols]
        w0 = lower(dot_abt(q[top, cols], k[top, cols]), 0)
        w1 = lower(dot_abt(q[low, cols], kh), half)
        att[top, cols] = dot_ab(w0, v[top, cols])
        att[low, cols] = dot_ab(w1, vh)
        w_top[head] = upper(dot_abt(k[top, cols], q[:, cols]))
        w_low[head] = upper(dot_abt(k[low, cols], q[low, cols]))
        return 0

    def beside(scan, unit, ahead, between):
        done = 0
        for j in range(chunks):
            for count, step in ((ahead if j else between, scan.gather), (between, scan.process)):
                upto = min(done + count, heads)
                if upto > done:
                    lax.fori_loop(done, upto, unit, 0)
                done = upto
                step(j)
        if heads > done:
            lax.fori_loop(done, heads, unit, 0)

    beside(scans[0], inside, 2, 1)
    loads[3].wait()

    sq[...] = jnp.zeros_like(sq)
    cr[...] = jnp.zeros_like(cr)

    def finish(head):
        cols = cols_of(head)
        a = att[:, cols] + dot_ab(q[:, cols], state_at(scans[0], head))
        att[:, cols] = a
        sq[...] += a * a
        cr[...] += a * (cot[:, cols].astype(F32) * gain_ref[:, cols])

    arrivals(scans[0], finish)

    lane = lax.broadcasted_iota(jnp.int32, sq.shape, 1)
    stats[mine] = jnp.where(
        lane < HEAD_DIM // 2,
        jnp.sum(sq[...], axis=1, keepdims=True),
        jnp.sum(cr[...], axis=1, keepdims=True),
    )

    def share(d, slot):
        return pltpu.make_async_remote_copy(
            src_ref=stats.at[mine],
            dst_ref=stats.at[slot],
            send_sem=f_send.at[d],
            recv_sem=f_recv.at[slot],
            device_id={"fsdp": lax.rem(mine + d, fs)},
            device_id_type=MESH,
        )

    for d in range(1, fs):
        share(d, mine).start()
    for d in range(1, fs):
        share(d, lax.rem(mine + d, fs)).wait_recv()
    both = stats[0]
    for f in range(1, fs):
        both = both + stats[f]
    inv = lax.rsqrt(both[:, 0:1] / HD + EPS)
    mean = both[:, HEAD_DIM - 1 : HEAD_DIM] * inv / HD
    sq[...] = jnp.broadcast_to(inv, sq.shape)
    cr[...] = jnp.broadcast_to(mean, cr.shape)

    def grad_state(head):
        cols = cols_of(head)
        up = cot[:, cols].astype(F32)
        normed = att[:, cols] * sq[...]
        gp[i, :, cols] = jnp.sum(up * normed, axis=0, keepdims=True)
        d_h = ((up * gain_ref[:, cols] - normed * cr[...]) * sq[...]).astype(BF16)
        do[:, cols] = d_h
        return dot_atb(q[:, cols], d_h)

    make_states(scans[1], grad_state)

    def gain_near(d, slot):
        return pltpu.make_async_remote_copy(
            src_ref=gp.at[i],
            dst_ref=gp.at[slot],
            send_sem=g_send.at[d],
            recv_sem=g_recv.at[slot],
            device_id={"seq": z * g + lax.rem(i + d, g)},
            device_id_type=MESH,
        )

    def gain_far(d, slot):
        return pltpu.make_async_remote_copy(
            src_ref=gz.at[z],
            dst_ref=gz.at[slot],
            send_sem=h_send.at[d],
            recv_sem=h_recv.at[slot],
            device_id={"seq": lax.rem(z + d, m) * g + i},
            device_id_type=MESH,
        )

    for d in range(1, g):
        gain_near(d, i).start()

    def backward(head, _):
        cols = cols_of(head)
        qh, kh, vh, dh = q[:, cols], k[:, cols], v[:, cols], do[:, cols]
        q1, k0, v0, d1 = q[low, cols], k[top, cols], v[top, cols], do[low, cols]
        from_prefix = dot_abt(dh, state_at(scans[0], head))
        s0 = lower(dot_abt(do[top, cols], v0), 0)
        s1 = lower(dot_abt(d1, vh), half)
        qg[top, cols] = (dot_ab(s0, k0) + from_prefix[:half]).astype(BF16)
        qg[low, cols] = (dot_ab(s1, kh) + from_prefix[half:]).astype(BF16)
        t0 = upper(dot_abt(v0, dh))
        t1 = upper(dot_abt(v[low, cols], d1))
        kg_l[top, cols] = dot_ab(t0, qh)
        kg_l[low, cols] = dot_ab(t1, q1)
        vg_l[top, cols] = dot_ab(w_top[head], dh)
        vg_l[low, cols] = dot_ab(w_low[head], d1)
        return 0

    beside(scans[1], backward, 1, 1)

    for d in range(1, g):
        gain_near(d, lax.rem(i + d, g)).wait_recv()
    near = gp[0]
    for p in range(1, g):
        near = near + gp[p]
    gz[z] = near
    for d in range(1, m):
        gain_far(d, z).start()

    def last(head):
        cols = cols_of(head)
        suffix = state_at(scans[1], head)
        kg[:, cols] = (kg_l[:, cols] + dot_abt(v[:, cols], suffix)).astype(BF16)
        vg[:, cols] = (vg_l[:, cols] + dot_ab(k[:, cols], suffix)).astype(BF16)

    arrivals(scans[1], last)

    for d in range(1, m):
        gain_far(d, lax.rem(z + d, m)).wait_recv()
    total = gz[0]
    for p in range(1, m):
        total = total + gz[p]
    gg_ref[...] = total * (1.0 / math.sqrt(rows * n))

    for scan in scans:
        scan.drain()
    for d in range(1, fs):
        share(d, mine).wait_send()
    for d in range(1, g):
        gain_near(d, i).wait_send()
    for d in range(1, m):
        gain_far(d, z).wait_send()


def store(qg, kg, vg, gg, qg_hbm, kg_hbm, vg_hbm, gg_hbm, sem):
    copies = [
        pltpu.make_async_copy(src, dst, sem.at[at])
        for at, (src, dst) in enumerate(((qg, qg_hbm), (kg, kg_hbm), (vg, vg_hbm), (gg, gg_hbm)))
    ]
    for copy in copies:
        copy.start()
    for copy in copies:
        copy.wait()


def solution(mesh):
    n, fs = mesh.shape["seq"], mesh.shape["fsdp"]
    g = group_size(n)
    m = n // g

    def shards(query, key, value, cotangent, gain):
        rows, width = query.shape
        heads = width // HEAD_DIM
        chunks = max(heads // g, 1)
        state = heads * HEAD_DIM
        piece = state // g
        levels = max(m.bit_length() - 1, 1)
        any_space = pl.BlockSpec(memory_space=pl.ANY)
        vmem = pl.BlockSpec(memory_space=pltpu.VMEM)
        dma = pltpu.SemaphoreType.DMA
        big, small = jax.ShapeDtypeStruct((rows, width), BF16), jax.ShapeDtypeStruct((1, width), F32)
        held = pltpu.VMEM((rows, width), BF16)
        products = 6 * rows * rows + 6 * rows * HEAD_DIM
        results = pl.pallas_call(
            functools.partial(kernel, n, g, fs, chunks),
            out_shape=(held, held, held, pltpu.VMEM((1, width), F32)),
            in_specs=[any_space] * 4 + [vmem],
            out_specs=(vmem, vmem, vmem, vmem),
            scratch_shapes=[pltpu.VMEM((rows, width), BF16)] * 5
            + [pltpu.VMEM((rows, width), F32)] * 3
            + [
                pltpu.VMEM((heads, rows // 2, rows), BF16),
                pltpu.VMEM((heads, rows // 2, rows // 2), BF16),
                pltpu.VMEM((2, state, HEAD_DIM), F32),
                pltpu.VMEM((2, g, piece, HEAD_DIM), F32),
                pltpu.VMEM((2, levels, piece, HEAD_DIM), F32),
                pltpu.VMEM((2, levels, piece, HEAD_DIM), F32),
                pltpu.VMEM((2, piece, HEAD_DIM), F32),
                pltpu.VMEM((2, g, piece, HEAD_DIM), F32),
                pltpu.VMEM((2, state, HEAD_DIM), F32),
                pltpu.VMEM((rows, HEAD_DIM), F32),
                pltpu.VMEM((rows, HEAD_DIM), F32),
                pltpu.VMEM((fs, rows, HEAD_DIM), F32),
                pltpu.VMEM((g, 1, width), F32),
                pltpu.VMEM((m, 1, width), F32),
                dma((4,)),
                dma((2, g, chunks)),
                dma((2, g, chunks)),
                dma((2, levels, max(m // 2, 1), chunks)),
                dma((2, levels, chunks)),
                dma((2, g, chunks)),
                dma((2, g, chunks)),
                dma((fs,)),
                dma((fs,)),
                dma((g,)),
                dma((g,)),
                dma((m,)),
                dma((m,)),
            ],
            compiler_params=pltpu.CompilerParams(
                collective_id=0, has_side_effects=True, vmem_limit_bytes=50 * 2**20
            ),
            cost_estimate=pl.CostEstimate(
                flops=2 * products * width, bytes_accessed=14 * rows * width, transcendentals=rows
            ),
        )(query, key, value, cotangent, gain.reshape(1, width))
        grads = pl.pallas_call(
            store,
            out_shape=(big, big, big, small),
            in_specs=[any_space] * 4,
            out_specs=(any_space,) * 4,
            scratch_shapes=[dma((4,))],
        )(*results)
        return (*grads[:3], grads[3].reshape(width))

    in_specs = (P("seq", "fsdp"), P("seq", "fsdp"), P("seq", "fsdp"), P("seq", "fsdp"), P("fsdp"))
    out_specs = (P("seq", "fsdp"), P("seq", "fsdp"), P("seq", "fsdp"), P("fsdp"))
    return jax.shard_map(shards, mesh=mesh, in_specs=in_specs, out_specs=out_specs, check_vma=False)
```

```python
import functools
import math

import jax
import jax.numpy as jnp
from jax import lax
from jax.experimental import pallas as pl
from jax.experimental.pallas import tpu as pltpu
from jax.sharding import PartitionSpec as P

HEAD_DIM = 128
HD = 4096
EPS = 1e-05
MESH = pl.DeviceIdType.MESH
F32 = jnp.float32
BF16 = jnp.bfloat16


def dot_ab(a, b):
    return lax.dot_general(a, b, (((1,), (0,)), ((), ())), preferred_element_type=F32)


def dot_abt(a, b):
    return lax.dot_general(a, b, (((1,), (1,)), ((), ())), preferred_element_type=F32)


def dot_atb(a, b):
    return lax.dot_general(a, b, (((0,), (0,)), ((), ())), preferred_element_type=F32)


def group_size(count):
    size = 1
    while size * size < count:
        size *= 2
    return size


def lower(block, offset):
    row = lax.broadcasted_iota(jnp.int32, block.shape, 0) + offset
    col = lax.broadcasted_iota(jnp.int32, block.shape, 1)
    return jnp.where(row >= col, block, 0.0).astype(BF16)


def upper(block):
    row = lax.broadcasted_iota(jnp.int32, block.shape, 0)
    col = lax.broadcasted_iota(jnp.int32, block.shape, 1)
    return jnp.where(row <= col, block, 0.0).astype(BF16)


def cols_of(head):
    return pl.ds(pl.multiple_of(head * HEAD_DIM, HEAD_DIM), HEAD_DIM)


class Scan:
    def __init__(self, which, reverse, g, m, chunks, refs, sems):
        self.which, self.reverse, self.g, self.m, self.chunks = which, reverse, g, m, chunks
        self.own, self.slots, self.carry, self.fwd, self.before, self.outs, self.result = refs
        self.a_send, self.a_recv, self.z_send, self.z_recv, self.b_send, self.b_recv = sems
        me = lax.axis_index("seq")
        self.z, self.i = me // g, lax.rem(me, g)
        self.piece = self.own.shape[0] // g
        self.ch = self.piece // chunks

    def peer(self, d):
        return lax.rem(self.i + d, self.g)

    def rows(self, p, j):
        return pl.ds(pl.multiple_of(p * self.piece + j * self.ch, self.ch), self.ch)

    def part(self, j):
        return pl.ds(pl.multiple_of(j * self.ch, self.ch), self.ch)

    def spread(self, d, j, arriving=False):
        p = self.peer(d)
        slot = p if arriving else self.i
        return pltpu.make_async_remote_copy(
            src_ref=self.own.at[self.rows(p, j)],
            dst_ref=self.slots.at[slot, self.part(j)],
            send_sem=self.a_send.at[self.which, d, j],
            recv_sem=self.a_recv.at[self.which, slot, j],
            device_id={"seq": self.z * self.g + p},
            device_id_type=MESH,
        )

    def place(self):
        return self.m - 1 - self.z if self.reverse else self.z

    def chain(self, level, t, j):
        place = jnp.clip(self.place() + 1 + t, 0, self.m - 1)
        group = self.m - 1 - place if self.reverse else place
        return pltpu.make_async_remote_copy(
            src_ref=self.fwd.at[level, self.part(j)],
            dst_ref=self.carry.at[level, self.part(j)],
            send_sem=self.z_send.at[self.which, level, t, j],
            recv_sem=self.z_recv.at[self.which, level, j],
            device_id={"seq": group * self.g + self.i},
            device_id_type=MESH,
        )

    def levels(self):
        return range(self.m.bit_length() - 1)

    def sends(self, level):
        return lax.rem(self.place(), 2 << level) == (1 << level) - 1

    def receives(self, level):
        return lax.rem(self.place(), 2 << level) >= 1 << level

    def forward(self, level, j, value):
        @pl.when(self.sends(level))
        def _():
            self.fwd[level, self.part(j)] = value()
            for t in range(1 << level):
                self.chain(level, t, j).start()

    def hand(self, d, j, arriving=False):
        p = self.peer(d)
        owner = p if arriving else self.i
        return pltpu.make_async_remote_copy(
            src_ref=self.outs.at[p, self.part(j)],
            dst_ref=self.result.at[self.rows(owner, j)],
            send_sem=self.b_send.at[self.which, d, j],
            recv_sem=self.b_recv.at[self.which, owner, j],
            device_id={"seq": self.z * self.g + p},
            device_id_type=MESH,
        )

    def total(self, j):
        total = self.slots[0, self.part(j)]
        for p in range(1, self.g):
            total = total + self.slots[p, self.part(j)]
        return total

    def gather(self, j):
        for d in range(1, self.g):
            self.spread(d, j, True).wait_recv()
        if self.m > 1:
            self.forward(0, j, lambda: self.total(j))

    def process(self, j):
        part = self.part(j)
        self.before[part] = jnp.zeros((self.ch, HEAD_DIM), F32)
        for level in self.levels():
            if level:
                self.forward(level, j, lambda: self.before[part] + self.total(j))

            @pl.when(self.receives(level))
            def _():
                self.chain(level, 0, j).wait_recv()
                self.before[part] += self.carry[level, part]

        running = self.before[part]
        order = range(self.g)
        for p in reversed(order) if self.reverse else order:
            self.outs[p, part] = running
            running = running + self.slots[p, part]
        for d in range(1, self.g):
            self.hand(d, j).start()
        self.result[self.rows(self.i, j)] = self.outs[self.i, part]

    def drain(self):
        def turn(j, _):
            for d in range(1, self.g):
                self.spread(d, j).wait_send()
                self.hand(d, j).wait_send()
            for level in self.levels():

                @pl.when(self.sends(level))
                def _():
                    for t in range(1 << level):
                        self.chain(level, t, j).wait_send()

            return 0

        lax.fori_loop(0, self.chunks, turn, 0)


def kernel(
    n, g, fs, chunks,
    q_hbm, k_hbm, v_hbm, c_hbm, gain_ref,
    qg, kg, vg, gg_ref,
    q, k, v, cot, do, att, kg_l, vg_l, w_top, w_low,
    own, slots, carry, fwd, before, outs, result,
    sq, cr, stats, gp, gz,
    in_sem, a_send, a_recv, z_send, z_recv, b_send, b_recv,
    f_send, f_recv, g_send, g_recv, h_send, h_recv,
):
    rows, width = q.shape
    heads = width // HEAD_DIM
    half = rows // 2
    m = n // g
    me = lax.axis_index("seq")
    mine = lax.axis_index("fsdp")
    z, i = me // g, lax.rem(me, g)

    loads = [
        pltpu.make_async_copy(src, dst, in_sem.at[at])
        for at, (src, dst) in enumerate(((k_hbm, k), (v_hbm, v), (q_hbm, q), (c_hbm, cot)))
    ]
    for load in loads:
        load.start()

    barrier = pltpu.get_barrier_semaphore()
    for d in range(1, g):
        pl.semaphore_signal(
            barrier, inc=1, device_id={"seq": z * g + lax.rem(i + d, g)}, device_id_type=MESH
        )
    for d in range(1, m):
        pl.semaphore_signal(
            barrier, inc=1, device_id={"seq": lax.rem(z + d, m) * g + i}, device_id_type=MESH
        )
    for d in range(1, fs):
        pl.semaphore_signal(
            barrier, inc=1, device_id={"fsdp": lax.rem(mine + d, fs)}, device_id_type=MESH
        )

    sems = (a_send, a_recv, z_send, z_recv, b_send, b_recv)
    scans = [
        Scan(w, w == 1, g, m, chunks, tuple(r.at[w] for r in (own, slots, carry, fwd, before, outs, result)), sems)
        for w in range(2)
    ]
    per = heads // g

    def make_states(scan, state_of):
        def turn(t, _):
            j, d = t // g, lax.rem(t + 1, g)
            p = scan.peer(d)
            state = state_of(p * per + j)
            scan.own[scan.rows(p, j)] = state

            @pl.when(d == 0)
            def _():
                scan.slots[i, scan.part(j)] = state

            @pl.when(d != 0)
            def _():
                scan.spread(d, j).start()

            return 0

        if per:
            lax.fori_loop(0, chunks * g, turn, 0)
        else:
            for head in range(heads):
                scan.own[pl.ds(head * HEAD_DIM, HEAD_DIM)] = state_of(head)
            for j in range(chunks):
                scan.slots[i, scan.part(j)] = scan.own[scan.rows(i, j)]
                for d in range(1, g):
                    scan.spread(d, j).start()

    def arrivals(scan, visit):
        def turn(t, _):
            j, d = t // g, lax.rem(t, g)

            @pl.when(d != 0)
            def _():
                scan.hand(d, j, True).wait_recv()

            visit(scan.peer(d) * per + j)
            return 0

        if per:
            lax.fori_loop(0, chunks * g, turn, 0)
        else:
            for j in range(chunks):
                for d in range(1, g):
                    scan.hand(d, j, True).wait_recv()
            for head in range(heads):
                visit(head)

    def state_at(scan, head):
        at = pl.ds(pl.multiple_of(head * HEAD_DIM, HEAD_DIM), HEAD_DIM)
        return scan.result[at].astype(BF16)

    loads[0].wait()
    loads[1].wait()
    pl.semaphore_wait(barrier, (g - 1) + (m - 1) + (fs - 1))
    make_states(scans[0], lambda head: dot_atb(k[:, cols_of(head)], v[:, cols_of(head)]))
    loads[2].wait()

    top, low = pl.ds(0, half), pl.ds(half, half)

    def inside(head):
        cols = cols_of(head)
        kh, vh = k[:, cols], v[:, cols]
        w0 = lower(dot_abt(q[top, cols], k[top, cols]), 0)
        w1 = lower(dot_abt(q[low, cols], kh), half)
        att[top, cols] = dot_ab(w0, v[top, cols])
        att[low, cols] = dot_ab(w1, vh)
        w_top[head] = upper(dot_abt(k[top, cols], q[:, cols]))
        w_low[head] = upper(dot_abt(k[low, cols], q[low, cols]))

    def beside(scan, unit, ahead, between):
        step = ahead + between

        def turn(u, _):
            unit(u)
            j = u // step

            @pl.when(jnp.logical_and(lax.rem(u, step) == ahead - 1, j < chunks))
            def _():
                scan.gather(j)

            @pl.when(jnp.logical_and(lax.rem(u, step) == step - 1, j < chunks))
            def _():
                scan.process(j)

            return 0

        if heads >= step * chunks:
            lax.fori_loop(0, heads, turn, 0)
        else:
            for head in range(heads):
                unit(head)
            for j in range(chunks):
                scan.gather(j)
                scan.process(j)

    beside(scans[0], inside, 2, 1)
    loads[3].wait()

    sq[...] = jnp.zeros_like(sq)
    cr[...] = jnp.zeros_like(cr)

    def finish(head):
        cols = cols_of(head)
        a = att[:, cols] + dot_ab(q[:, cols], state_at(scans[0], head))
        att[:, cols] = a
        sq[...] += a * a
        cr[...] += a * (cot[:, cols].astype(F32) * gain_ref[:, cols])

    arrivals(scans[0], finish)

    lane = lax.broadcasted_iota(jnp.int32, sq.shape, 1)
    stats[mine] = jnp.where(
        lane < HEAD_DIM // 2,
        jnp.sum(sq[...], axis=1, keepdims=True),
        jnp.sum(cr[...], axis=1, keepdims=True),
    )

    def share(d, slot):
        return pltpu.make_async_remote_copy(
            src_ref=stats.at[mine],
            dst_ref=stats.at[slot],
            send_sem=f_send.at[d],
            recv_sem=f_recv.at[slot],
            device_id={"fsdp": lax.rem(mine + d, fs)},
            device_id_type=MESH,
        )

    for d in range(1, fs):
        share(d, mine).start()
    for d in range(1, fs):
        share(d, lax.rem(mine + d, fs)).wait_recv()
    both = stats[0]
    for f in range(1, fs):
        both = both + stats[f]
    inv = lax.rsqrt(both[:, 0:1] / HD + EPS)
    mean = both[:, HEAD_DIM - 1 : HEAD_DIM] * inv / HD
    sq[...] = jnp.broadcast_to(inv, sq.shape)
    cr[...] = jnp.broadcast_to(mean, cr.shape)

    def grad_state(head):
        cols = cols_of(head)
        up = cot[:, cols].astype(F32)
        normed = att[:, cols] * sq[...]
        gp[i, :, cols] = jnp.sum(up * normed, axis=0, keepdims=True)
        d_h = ((up * gain_ref[:, cols] - normed * cr[...]) * sq[...]).astype(BF16)
        do[:, cols] = d_h
        return dot_atb(q[:, cols], d_h)

    make_states(scans[1], grad_state)

    def gain_near(d, slot):
        return pltpu.make_async_remote_copy(
            src_ref=gp.at[i],
            dst_ref=gp.at[slot],
            send_sem=g_send.at[d],
            recv_sem=g_recv.at[slot],
            device_id={"seq": z * g + lax.rem(i + d, g)},
            device_id_type=MESH,
        )

    def gain_far(d, slot):
        return pltpu.make_async_remote_copy(
            src_ref=gz.at[z],
            dst_ref=gz.at[slot],
            send_sem=h_send.at[d],
            recv_sem=h_recv.at[slot],
            device_id={"seq": lax.rem(z + d, m) * g + i},
            device_id_type=MESH,
        )

    for d in range(1, g):
        gain_near(d, i).start()

    def backward(head):
        cols = cols_of(head)
        qh, kh, vh, dh = q[:, cols], k[:, cols], v[:, cols], do[:, cols]
        q1, k0, v0, d1 = q[low, cols], k[top, cols], v[top, cols], do[low, cols]
        from_prefix = dot_abt(dh, state_at(scans[0], head))
        s0 = lower(dot_abt(do[top, cols], v0), 0)
        s1 = lower(dot_abt(d1, vh), half)
        qg[top, cols] = (dot_ab(s0, k0) + from_prefix[:half]).astype(BF16)
        qg[low, cols] = (dot_ab(s1, kh) + from_prefix[half:]).astype(BF16)
        t0 = upper(dot_abt(v0, dh))
        t1 = upper(dot_abt(v[low, cols], d1))
        kg_l[top, cols] = dot_ab(t0, qh)
        kg_l[low, cols] = dot_ab(t1, q1)
        vg_l[top, cols] = dot_ab(w_top[head], dh)
        vg_l[low, cols] = dot_ab(w_low[head], d1)

    beside(scans[1], backward, 1, 1)

    for d in range(1, g):
        gain_near(d, lax.rem(i + d, g)).wait_recv()
    near = gp[0]
    for p in range(1, g):
        near = near + gp[p]
    gz[z] = near
    for d in range(1, m):
        gain_far(d, z).start()

    def last(head):
        cols = cols_of(head)
        suffix = state_at(scans[1], head)
        kg[:, cols] = (kg_l[:, cols] + dot_abt(v[:, cols], suffix)).astype(BF16)
        vg[:, cols] = (vg_l[:, cols] + dot_ab(k[:, cols], suffix)).astype(BF16)

    arrivals(scans[1], last)

    for d in range(1, m):
        gain_far(d, lax.rem(z + d, m)).wait_recv()
    total = gz[0]
    for p in range(1, m):
        total = total + gz[p]
    gg_ref[...] = total * (1.0 / math.sqrt(rows * n))

    for scan in scans:
        scan.drain()
    for d in range(1, fs):
        share(d, mine).wait_send()
    for d in range(1, g):
        gain_near(d, i).wait_send()
    for d in range(1, m):
        gain_far(d, z).wait_send()


def store(qg, kg, vg, gg, qg_hbm, kg_hbm, vg_hbm, gg_hbm, sem):
    copies = [
        pltpu.make_async_copy(src, dst, sem.at[at])
        for at, (src, dst) in enumerate(((qg, qg_hbm), (kg, kg_hbm), (vg, vg_hbm), (gg, gg_hbm)))
    ]
    for copy in copies:
        copy.start()
    for copy in copies:
        copy.wait()


def solution(mesh):
    n, fs = mesh.shape["seq"], mesh.shape["fsdp"]
    g = group_size(n)
    m = n // g

    def shards(query, key, value, cotangent, gain):
        rows, width = query.shape
        heads = width // HEAD_DIM
        chunks = max(heads // g, 1)
        state = heads * HEAD_DIM
        piece = state // g
        levels = max(m.bit_length() - 1, 1)
        any_space = pl.BlockSpec(memory_space=pl.ANY)
        vmem = pl.BlockSpec(memory_space=pltpu.VMEM)
        dma = pltpu.SemaphoreType.DMA
        big, small = jax.ShapeDtypeStruct((rows, width), BF16), jax.ShapeDtypeStruct((1, width), F32)
        held = pltpu.VMEM((rows, width), BF16)
        products = 6 * rows * rows + 6 * rows * HEAD_DIM
        results = pl.pallas_call(
            functools.partial(kernel, n, g, fs, chunks),
            out_shape=(held, held, held, pltpu.VMEM((1, width), F32)),
            in_specs=[any_space] * 4 + [vmem],
            out_specs=(vmem, vmem, vmem, vmem),
            scratch_shapes=[pltpu.VMEM((rows, width), BF16)] * 5
            + [pltpu.VMEM((rows, width), F32)] * 3
            + [
                pltpu.VMEM((heads, rows // 2, rows), BF16),
                pltpu.VMEM((heads, rows // 2, rows // 2), BF16),
                pltpu.VMEM((2, state, HEAD_DIM), F32),
                pltpu.VMEM((2, g, piece, HEAD_DIM), F32),
                pltpu.VMEM((2, levels, piece, HEAD_DIM), F32),
                pltpu.VMEM((2, levels, piece, HEAD_DIM), F32),
                pltpu.VMEM((2, piece, HEAD_DIM), F32),
                pltpu.VMEM((2, g, piece, HEAD_DIM), F32),
                pltpu.VMEM((2, state, HEAD_DIM), F32),
                pltpu.VMEM((rows, HEAD_DIM), F32),
                pltpu.VMEM((rows, HEAD_DIM), F32),
                pltpu.VMEM((fs, rows, HEAD_DIM), F32),
                pltpu.VMEM((g, 1, width), F32),
                pltpu.VMEM((m, 1, width), F32),
                dma((4,)),
                dma((2, g, chunks)),
                dma((2, g, chunks)),
                dma((2, levels, max(m // 2, 1), chunks)),
                dma((2, levels, chunks)),
                dma((2, g, chunks)),
                dma((2, g, chunks)),
                dma((fs,)),
                dma((fs,)),
                dma((g,)),
                dma((g,)),
                dma((m,)),
                dma((m,)),
            ],
            compiler_params=pltpu.CompilerParams(
                collective_id=0, has_side_effects=True, vmem_limit_bytes=50 * 2**20
            ),
            cost_estimate=pl.CostEstimate(
                flops=2 * products * width, bytes_accessed=14 * rows * width, transcendentals=rows
            ),
        )(query, key, value, cotangent, gain.reshape(1, width))
        grads = pl.pallas_call(
            store,
            out_shape=(big, big, big, small),
            in_specs=[any_space] * 4,
            out_specs=(any_space,) * 4,
            scratch_shapes=[dma((4,))],
            compiler_params=pltpu.CompilerParams(vmem_limit_bytes=2**20),
        )(*results)
        return (*grads[:3], grads[3].reshape(width))

    in_specs = (P("seq", "fsdp"), P("seq", "fsdp"), P("seq", "fsdp"), P("seq", "fsdp"), P("fsdp"))
    out_specs = (P("seq", "fsdp"), P("seq", "fsdp"), P("seq", "fsdp"), P("fsdp"))
    return jax.shard_map(shards, mesh=mesh, in_specs=in_specs, out_specs=out_specs, check_vma=False)
```

```python
import functools
import math

import jax
import jax.numpy as jnp
from jax import lax
from jax.experimental import pallas as pl
from jax.experimental.pallas import tpu as pltpu
from jax.sharding import PartitionSpec as P

HEAD_DIM = 128
HD = 4096
EPS = 1e-05
MESH = pl.DeviceIdType.MESH
F32 = jnp.float32
BF16 = jnp.bfloat16


def dot_ab(a, b):
    return lax.dot_general(a, b, (((1,), (0,)), ((), ())), preferred_element_type=F32)


def dot_abt(a, b):
    return lax.dot_general(a, b, (((1,), (1,)), ((), ())), preferred_element_type=F32)


def dot_atb(a, b):
    return lax.dot_general(a, b, (((0,), (0,)), ((), ())), preferred_element_type=F32)


def group_size(count):
    size = 1
    while size * size < count:
        size *= 2
    return size


def lower(block):
    row = lax.broadcasted_iota(jnp.int32, block.shape, 0)
    col = lax.broadcasted_iota(jnp.int32, block.shape, 1)
    return jnp.where(row >= col, block, 0.0).astype(BF16)


def upper(block):
    row = lax.broadcasted_iota(jnp.int32, block.shape, 0)
    col = lax.broadcasted_iota(jnp.int32, block.shape, 1)
    return jnp.where(row <= col, block, 0.0).astype(BF16)


def cols_of(head):
    return pl.ds(pl.multiple_of(head * HEAD_DIM, HEAD_DIM), HEAD_DIM)


def bottom(left, right):
    return jnp.concatenate([left.astype(BF16), lower(right)], axis=1)


def top_of(left, right):
    return jnp.concatenate([upper(left), right.astype(BF16)], axis=1)


class Scan:
    def __init__(self, which, reverse, g, m, chunks, refs, sems):
        self.which, self.reverse, self.g, self.m, self.chunks = which, reverse, g, m, chunks
        self.own, self.slots, self.carry, self.fwd, self.before, self.outs, self.result = refs
        self.a_send, self.a_recv, self.z_send, self.z_recv, self.b_send, self.b_recv = sems
        me = lax.axis_index("seq")
        self.z, self.i = me // g, lax.rem(me, g)
        self.piece = self.own.shape[0] // g
        self.ch = self.piece // chunks

    def peer(self, d):
        return lax.rem(self.i + d, self.g)

    def rows(self, p, j):
        return pl.ds(pl.multiple_of(p * self.piece + j * self.ch, self.ch), self.ch)

    def part(self, j):
        return pl.ds(pl.multiple_of(j * self.ch, self.ch), self.ch)

    def spread(self, d, j, arriving=False):
        p = self.peer(d)
        slot = p if arriving else self.i
        return pltpu.make_async_remote_copy(
            src_ref=self.own.at[self.rows(p, j)],
            dst_ref=self.slots.at[slot, self.part(j)],
            send_sem=self.a_send.at[self.which, d, j],
            recv_sem=self.a_recv.at[self.which, slot, j],
            device_id={"seq": self.z * self.g + p},
            device_id_type=MESH,
        )

    def place(self):
        return self.m - 1 - self.z if self.reverse else self.z

    def chain(self, level, t, j):
        place = jnp.clip(self.place() + 1 + t, 0, self.m - 1)
        group = self.m - 1 - place if self.reverse else place
        return pltpu.make_async_remote_copy(
            src_ref=self.fwd.at[level, self.part(j)],
            dst_ref=self.carry.at[level, self.part(j)],
            send_sem=self.z_send.at[self.which, level, t, j],
            recv_sem=self.z_recv.at[self.which, level, j],
            device_id={"seq": group * self.g + self.i},
            device_id_type=MESH,
        )

    def levels(self):
        return range(self.m.bit_length() - 1)

    def sends(self, level):
        return lax.rem(self.place(), 2 << level) == (1 << level) - 1

    def receives(self, level):
        return lax.rem(self.place(), 2 << level) >= 1 << level

    def forward(self, level, j, value):
        @pl.when(self.sends(level))
        def _():
            self.fwd[level, self.part(j)] = value()
            for t in range(1 << level):
                self.chain(level, t, j).start()

    def hand(self, d, j, arriving=False):
        p = self.peer(d)
        owner = p if arriving else self.i
        return pltpu.make_async_remote_copy(
            src_ref=self.outs.at[p, self.part(j)],
            dst_ref=self.result.at[self.rows(owner, j)],
            send_sem=self.b_send.at[self.which, d, j],
            recv_sem=self.b_recv.at[self.which, owner, j],
            device_id={"seq": self.z * self.g + p},
            device_id_type=MESH,
        )

    def total(self, j):
        total = self.slots[0, self.part(j)]
        for p in range(1, self.g):
            total = total + self.slots[p, self.part(j)]
        return total

    def gather(self, j):
        for d in range(1, self.g):
            self.spread(d, j, True).wait_recv()
        if self.m > 1:
            self.forward(0, j, lambda: self.total(j))

    def process(self, j):
        part = self.part(j)
        self.before[part] = jnp.zeros((self.ch, HEAD_DIM), F32)
        for level in self.levels():
            if level:
                self.forward(level, j, lambda: self.before[part] + self.total(j))

            @pl.when(self.receives(level))
            def _():
                self.chain(level, 0, j).wait_recv()
                self.before[part] += self.carry[level, part]

        running = self.before[part]
        order = range(self.g)
        for p in reversed(order) if self.reverse else order:
            self.outs[p, part] = running
            running = running + self.slots[p, part]
        for d in range(1, self.g):
            self.hand(d, j).start()
        self.result[self.rows(self.i, j)] = self.outs[self.i, part]

    def drain(self):
        def turn(j, _):
            for d in range(1, self.g):
                self.spread(d, j).wait_send()
                self.hand(d, j).wait_send()
            for level in self.levels():

                @pl.when(self.sends(level))
                def _():
                    for t in range(1 << level):
                        self.chain(level, t, j).wait_send()

            return 0

        lax.fori_loop(0, self.chunks, turn, 0)


def kernel(
    n, g, fs, chunks,
    q_hbm, k_hbm, v_hbm, c_hbm, gain_ref,
    qg, kg, vg, gg_ref,
    q, k, v, cot, do, att, kg_l, vg_l, w_top, w_low,
    own, slots, carry, fwd, before, outs, result,
    sq, cr, stats, gp, gz,
    in_sem, a_send, a_recv, z_send, z_recv, b_send, b_recv,
    f_send, f_recv, g_send, g_recv, h_send, h_recv,
):
    rows, width = q.shape
    heads = width // HEAD_DIM
    half = rows // 2
    m = n // g
    me = lax.axis_index("seq")
    mine = lax.axis_index("fsdp")
    z, i = me // g, lax.rem(me, g)

    loads = [
        pltpu.make_async_copy(src, dst, in_sem.at[at])
        for at, (src, dst) in enumerate(((k_hbm, k), (v_hbm, v), (q_hbm, q), (c_hbm, cot)))
    ]
    for load in loads:
        load.start()

    barrier = pltpu.get_barrier_semaphore()
    for d in range(1, g):
        pl.semaphore_signal(
            barrier, inc=1, device_id={"seq": z * g + lax.rem(i + d, g)}, device_id_type=MESH
        )
    for d in range(1, m):
        pl.semaphore_signal(
            barrier, inc=1, device_id={"seq": lax.rem(z + d, m) * g + i}, device_id_type=MESH
        )
    for d in range(1, fs):
        pl.semaphore_signal(
            barrier, inc=1, device_id={"fsdp": lax.rem(mine + d, fs)}, device_id_type=MESH
        )

    sems = (a_send, a_recv, z_send, z_recv, b_send, b_recv)
    scans = [
        Scan(w, w == 1, g, m, chunks, tuple(r.at[w] for r in (own, slots, carry, fwd, before, outs, result)), sems)
        for w in range(2)
    ]
    per = heads // g

    def make_states(scan, state_of):
        def turn(t, _):
            j, d = t // g, lax.rem(t + 1, g)
            p = scan.peer(d)
            state = state_of(p * per + j)
            scan.own[scan.rows(p, j)] = state

            @pl.when(d == 0)
            def _():
                scan.slots[i, scan.part(j)] = state

            @pl.when(d != 0)
            def _():
                scan.spread(d, j).start()

            return 0

        if per:
            lax.fori_loop(0, chunks * g, turn, 0)
        else:
            for head in range(heads):
                scan.own[pl.ds(head * HEAD_DIM, HEAD_DIM)] = state_of(head)
            for j in range(chunks):
                scan.slots[i, scan.part(j)] = scan.own[scan.rows(i, j)]
                for d in range(1, g):
                    scan.spread(d, j).start()

    def arrivals(scan, visit):
        def turn(t, _):
            j, d = t // g, lax.rem(t, g)

            @pl.when(d != 0)
            def _():
                scan.hand(d, j, True).wait_recv()

            visit(scan.peer(d) * per + j)
            return 0

        if per:
            lax.fori_loop(0, chunks * g, turn, 0)
        else:
            for j in range(chunks):
                for d in range(1, g):
                    scan.hand(d, j, True).wait_recv()
            for head in range(heads):
                visit(head)

    def state_at(scan, head):
        at = pl.ds(pl.multiple_of(head * HEAD_DIM, HEAD_DIM), HEAD_DIM)
        return scan.result[at].astype(BF16)

    loads[0].wait()
    loads[1].wait()
    pl.semaphore_wait(barrier, (g - 1) + (m - 1) + (fs - 1))
    make_states(scans[0], lambda head: dot_atb(k[:, cols_of(head)], v[:, cols_of(head)]))
    loads[2].wait()

    top, low = pl.ds(0, half), pl.ds(half, half)

    def inside(head):
        cols = cols_of(head)
        vh = v[:, cols]
        q0, q1, k0, k1 = q[top, cols], q[low, cols], k[top, cols], k[low, cols]
        w0 = lower(dot_abt(q0, k0))
        w1 = bottom(dot_abt(q1, k0), dot_abt(q1, k1))
        att[top, cols] = dot_ab(w0, v[top, cols])
        att[low, cols] = dot_ab(w1, vh)
        w_top[head] = top_of(dot_abt(k0, q0), dot_abt(k0, q1))
        w_low[head] = upper(dot_abt(k1, q1))

    def beside(scan, unit, width):
        def turn(u, _):
            for at in range(width):
                unit(u * width + at)

            @pl.when(u < chunks)
            def _():
                scan.gather(u)
                scan.process(u)

            return 0

        if heads >= width * chunks and heads % width == 0:
            lax.fori_loop(0, heads // width, turn, 0)
        else:
            for head in range(heads):
                unit(head)
            for j in range(chunks):
                scan.gather(j)
                scan.process(j)

    beside(scans[0], inside, 2)
    loads[3].wait()

    sq[...] = jnp.zeros_like(sq)
    cr[...] = jnp.zeros_like(cr)

    def finish(head):
        cols = cols_of(head)
        a = att[:, cols] + dot_ab(q[:, cols], state_at(scans[0], head))
        att[:, cols] = a
        sq[...] += a * a
        cr[...] += a * (cot[:, cols].astype(F32) * gain_ref[:, cols])

    arrivals(scans[0], finish)

    lane = lax.broadcasted_iota(jnp.int32, sq.shape, 1)
    stats[mine] = jnp.where(
        lane < HEAD_DIM // 2,
        jnp.sum(sq[...], axis=1, keepdims=True),
        jnp.sum(cr[...], axis=1, keepdims=True),
    )

    def share(d, slot):
        return pltpu.make_async_remote_copy(
            src_ref=stats.at[mine],
            dst_ref=stats.at[slot],
            send_sem=f_send.at[d],
            recv_sem=f_recv.at[slot],
            device_id={"fsdp": lax.rem(mine + d, fs)},
            device_id_type=MESH,
        )

    for d in range(1, fs):
        share(d, mine).start()
    for d in range(1, fs):
        share(d, lax.rem(mine + d, fs)).wait_recv()
    both = stats[0]
    for f in range(1, fs):
        both = both + stats[f]
    inv = lax.rsqrt(both[:, 0:1] / HD + EPS)
    mean = both[:, HEAD_DIM - 1 : HEAD_DIM] * inv / HD
    sq[...] = jnp.broadcast_to(inv, sq.shape)
    cr[...] = jnp.broadcast_to(mean, cr.shape)

    def grad_state(head):
        cols = cols_of(head)
        up = cot[:, cols].astype(F32)
        normed = att[:, cols] * sq[...]
        gp[i, :, cols] = jnp.sum(up * normed, axis=0, keepdims=True)
        d_h = ((up * gain_ref[:, cols] - normed * cr[...]) * sq[...]).astype(BF16)
        do[:, cols] = d_h
        return dot_atb(q[:, cols], d_h)

    make_states(scans[1], grad_state)

    def gain_near(d, slot):
        return pltpu.make_async_remote_copy(
            src_ref=gp.at[i],
            dst_ref=gp.at[slot],
            send_sem=g_send.at[d],
            recv_sem=g_recv.at[slot],
            device_id={"seq": z * g + lax.rem(i + d, g)},
            device_id_type=MESH,
        )

    def gain_far(d, slot):
        return pltpu.make_async_remote_copy(
            src_ref=gz.at[z],
            dst_ref=gz.at[slot],
            send_sem=h_send.at[d],
            recv_sem=h_recv.at[slot],
            device_id={"seq": lax.rem(z + d, m) * g + i},
            device_id_type=MESH,
        )

    for d in range(1, g):
        gain_near(d, i).start()

    def backward(head):
        cols = cols_of(head)
        qh, kh, dh = q[:, cols], k[:, cols], do[:, cols]
        q1, k0, v0, v1 = q[low, cols], k[top, cols], v[top, cols], v[low, cols]
        d0, d1 = do[top, cols], do[low, cols]
        from_prefix = dot_abt(dh, state_at(scans[0], head))
        s0 = lower(dot_abt(d0, v0))
        s1 = bottom(dot_abt(d1, v0), dot_abt(d1, v1))
        qg[top, cols] = (dot_ab(s0, k0) + from_prefix[:half]).astype(BF16)
        qg[low, cols] = (dot_ab(s1, kh) + from_prefix[half:]).astype(BF16)
        t0 = top_of(dot_abt(v0, d0), dot_abt(v0, d1))
        t1 = upper(dot_abt(v1, d1))
        kg_l[top, cols] = dot_ab(t0, qh)
        kg_l[low, cols] = dot_ab(t1, q1)
        vg_l[top, cols] = dot_ab(w_top[head], dh)
        vg_l[low, cols] = dot_ab(w_low[head], d1)

    beside(scans[1], backward, 2)

    for d in range(1, g):
        gain_near(d, lax.rem(i + d, g)).wait_recv()
    near = gp[0]
    for p in range(1, g):
        near = near + gp[p]
    gz[z] = near
    for d in range(1, m):
        gain_far(d, z).start()

    def last(head):
        cols = cols_of(head)
        suffix = state_at(scans[1], head)
        kg[:, cols] = (kg_l[:, cols] + dot_abt(v[:, cols], suffix)).astype(BF16)
        vg[:, cols] = (vg_l[:, cols] + dot_ab(k[:, cols], suffix)).astype(BF16)

    arrivals(scans[1], last)

    for d in range(1, m):
        gain_far(d, lax.rem(z + d, m)).wait_recv()
    total = gz[0]
    for p in range(1, m):
        total = total + gz[p]
    gg_ref[...] = total * (1.0 / math.sqrt(rows * n))

    for scan in scans:
        scan.drain()
    for d in range(1, fs):
        share(d, mine).wait_send()
    for d in range(1, g):
        gain_near(d, i).wait_send()
    for d in range(1, m):
        gain_far(d, z).wait_send()


def store(qg, kg, vg, gg, qg_hbm, kg_hbm, vg_hbm, gg_hbm, sem):
    copies = [
        pltpu.make_async_copy(src, dst, sem.at[at])
        for at, (src, dst) in enumerate(((qg, qg_hbm), (kg, kg_hbm), (vg, vg_hbm), (gg, gg_hbm)))
    ]
    for copy in copies:
        copy.start()
    for copy in copies:
        copy.wait()


def solution(mesh):
    n, fs = mesh.shape["seq"], mesh.shape["fsdp"]
    g = group_size(n)
    m = n // g

    def shards(query, key, value, cotangent, gain):
        rows, width = query.shape
        heads = width // HEAD_DIM
        chunks = max(heads // g, 1)
        state = heads * HEAD_DIM
        piece = state // g
        levels = max(m.bit_length() - 1, 1)
        any_space = pl.BlockSpec(memory_space=pl.ANY)
        vmem = pl.BlockSpec(memory_space=pltpu.VMEM)
        dma = pltpu.SemaphoreType.DMA
        big, small = jax.ShapeDtypeStruct((rows, width), BF16), jax.ShapeDtypeStruct((1, width), F32)
        held = pltpu.VMEM((rows, width), BF16)
        products = 6 * rows * rows + 6 * rows * HEAD_DIM
        results = pl.pallas_call(
            functools.partial(kernel, n, g, fs, chunks),
            out_shape=(held, held, held, pltpu.VMEM((1, width), F32)),
            in_specs=[any_space] * 4 + [vmem],
            out_specs=(vmem, vmem, vmem, vmem),
            scratch_shapes=[pltpu.VMEM((rows, width), BF16)] * 5
            + [pltpu.VMEM((rows, width), F32)] * 3
            + [
                pltpu.VMEM((heads, rows // 2, rows), BF16),
                pltpu.VMEM((heads, rows // 2, rows // 2), BF16),
                pltpu.VMEM((2, state, HEAD_DIM), F32),
                pltpu.VMEM((2, g, piece, HEAD_DIM), F32),
                pltpu.VMEM((2, levels, piece, HEAD_DIM), F32),
                pltpu.VMEM((2, levels, piece, HEAD_DIM), F32),
                pltpu.VMEM((2, piece, HEAD_DIM), F32),
                pltpu.VMEM((2, g, piece, HEAD_DIM), F32),
                pltpu.VMEM((2, state, HEAD_DIM), F32),
                pltpu.VMEM((rows, HEAD_DIM), F32),
                pltpu.VMEM((rows, HEAD_DIM), F32),
                pltpu.VMEM((fs, rows, HEAD_DIM), F32),
                pltpu.VMEM((g, 1, width), F32),
                pltpu.VMEM((m, 1, width), F32),
                dma((4,)),
                dma((2, g, chunks)),
                dma((2, g, chunks)),
                dma((2, levels, max(m // 2, 1), chunks)),
                dma((2, levels, chunks)),
                dma((2, g, chunks)),
                dma((2, g, chunks)),
                dma((fs,)),
                dma((fs,)),
                dma((g,)),
                dma((g,)),
                dma((m,)),
                dma((m,)),
            ],
            compiler_params=pltpu.CompilerParams(
                collective_id=0, has_side_effects=True, vmem_limit_bytes=50 * 2**20
            ),
            cost_estimate=pl.CostEstimate(
                flops=2 * products * width, bytes_accessed=14 * rows * width, transcendentals=rows
            ),
        )(query, key, value, cotangent, gain.reshape(1, width))
        grads = pl.pallas_call(
            store,
            out_shape=(big, big, big, small),
            in_specs=[any_space] * 4,
            out_specs=(any_space,) * 4,
            scratch_shapes=[dma((4,))],
            compiler_params=pltpu.CompilerParams(vmem_limit_bytes=2**20),
        )(*results)
        return (*grads[:3], grads[3].reshape(width))

    in_specs = (P("seq", "fsdp"), P("seq", "fsdp"), P("seq", "fsdp"), P("seq", "fsdp"), P("fsdp"))
    out_specs = (P("seq", "fsdp"), P("seq", "fsdp"), P("seq", "fsdp"), P("fsdp"))
    return jax.shard_map(shards, mesh=mesh, in_specs=in_specs, out_specs=out_specs, check_vma=False)
```

```python
import functools
import math

import jax
import jax.numpy as jnp
from jax import lax
from jax.experimental import pallas as pl
from jax.experimental.pallas import tpu as pltpu
from jax.sharding import PartitionSpec as P

HEAD_DIM = 128
HD = 4096
EPS = 1e-05
MESH = pl.DeviceIdType.MESH
F32 = jnp.float32
BF16 = jnp.bfloat16


def dot_ab(a, b):
    return lax.dot_general(a, b, (((1,), (0,)), ((), ())), preferred_element_type=F32)


def dot_abt(a, b):
    return lax.dot_general(a, b, (((1,), (1,)), ((), ())), preferred_element_type=F32)


def dot_atb(a, b):
    return lax.dot_general(a, b, (((0,), (0,)), ((), ())), preferred_element_type=F32)


def group_size(count):
    size = 1
    while size * size < count:
        size *= 2
    return size


def lower(block):
    row = lax.broadcasted_iota(jnp.int32, block.shape, 0)
    col = lax.broadcasted_iota(jnp.int32, block.shape, 1)
    return jnp.where(row >= col, block, 0.0).astype(BF16)


def upper(block):
    row = lax.broadcasted_iota(jnp.int32, block.shape, 0)
    col = lax.broadcasted_iota(jnp.int32, block.shape, 1)
    return jnp.where(row <= col, block, 0.0).astype(BF16)


def cols_of(head):
    return pl.ds(pl.multiple_of(head * HEAD_DIM, HEAD_DIM), HEAD_DIM)


def bottom(left, right):
    return jnp.concatenate([left.astype(BF16), lower(right)], axis=1)


def top_of(left, right):
    return jnp.concatenate([upper(left), right.astype(BF16)], axis=1)


class Scan:
    def __init__(self, which, reverse, g, m, chunks, refs, sems):
        self.which, self.reverse, self.g, self.m, self.chunks = which, reverse, g, m, chunks
        self.own, self.slots, self.carry, self.fwd, self.before, self.outs, self.result = refs
        self.a_send, self.a_recv, self.z_send, self.z_recv, self.b_send, self.b_recv = sems
        me = lax.axis_index("seq")
        self.z, self.i = me // g, lax.rem(me, g)
        self.piece = self.own.shape[0] // g
        self.ch = self.piece // chunks

    def peer(self, d):
        return lax.rem(self.i + d, self.g)

    def rows(self, p, j):
        return pl.ds(pl.multiple_of(p * self.piece + j * self.ch, self.ch), self.ch)

    def part(self, j):
        return pl.ds(pl.multiple_of(j * self.ch, self.ch), self.ch)

    def spread(self, d, j, arriving=False):
        p = self.peer(d)
        slot = p if arriving else self.i
        return pltpu.make_async_remote_copy(
            src_ref=self.own.at[self.rows(p, j)],
            dst_ref=self.slots.at[slot, self.part(j)],
            send_sem=self.a_send.at[self.which, d, j],
            recv_sem=self.a_recv.at[self.which, slot, j],
            device_id={"seq": self.z * self.g + p},
            device_id_type=MESH,
        )

    def place(self):
        return self.m - 1 - self.z if self.reverse else self.z

    def chain(self, level, t, j):
        place = jnp.clip(self.place() + 1 + t, 0, self.m - 1)
        group = self.m - 1 - place if self.reverse else place
        return pltpu.make_async_remote_copy(
            src_ref=self.fwd.at[level, self.part(j)],
            dst_ref=self.carry.at[level, self.part(j)],
            send_sem=self.z_send.at[self.which, level, t, j],
            recv_sem=self.z_recv.at[self.which, level, j],
            device_id={"seq": group * self.g + self.i},
            device_id_type=MESH,
        )

    def levels(self):
        return range(self.m.bit_length() - 1)

    def sends(self, level):
        return lax.rem(self.place(), 2 << level) == (1 << level) - 1

    def receives(self, level):
        return lax.rem(self.place(), 2 << level) >= 1 << level

    def forward(self, level, j, value):
        @pl.when(self.sends(level))
        def _():
            self.fwd[level, self.part(j)] = value()
            for t in range(1 << level):
                self.chain(level, t, j).start()

    def hand(self, d, j, arriving=False):
        p = self.peer(d)
        owner = p if arriving else self.i
        return pltpu.make_async_remote_copy(
            src_ref=self.outs.at[p, self.part(j)],
            dst_ref=self.result.at[self.rows(owner, j)],
            send_sem=self.b_send.at[self.which, d, j],
            recv_sem=self.b_recv.at[self.which, owner, j],
            device_id={"seq": self.z * self.g + p},
            device_id_type=MESH,
        )

    def total(self, j):
        total = self.slots[0, self.part(j)]
        for p in range(1, self.g):
            total = total + self.slots[p, self.part(j)]
        return total

    def gather(self, j):
        for d in range(1, self.g):
            self.spread(d, j, True).wait_recv()
        if self.m > 1:
            self.forward(0, j, lambda: self.total(j))

    def process(self, j):
        part = self.part(j)
        self.before[part] = jnp.zeros((self.ch, HEAD_DIM), F32)
        for level in self.levels():
            if level:
                self.forward(level, j, lambda: self.before[part] + self.total(j))

            @pl.when(self.receives(level))
            def _():
                self.chain(level, 0, j).wait_recv()
                self.before[part] += self.carry[level, part]

        running = self.before[part]
        order = range(self.g)
        for p in reversed(order) if self.reverse else order:
            self.outs[p, part] = running
            running = running + self.slots[p, part]
        for d in range(1, self.g):
            self.hand(d, j).start()
        self.result[self.rows(self.i, j)] = self.outs[self.i, part]

    def sent(self, j):
        for d in range(1, self.g):
            self.spread(d, j).wait_send()

    def drain(self, unsent):
        for j in range(self.chunks - unsent, self.chunks):
            self.sent(j)

        def turn(j, _):
            for d in range(1, self.g):
                self.hand(d, j).wait_send()
            for level in self.levels():

                @pl.when(self.sends(level))
                def _():
                    for t in range(1 << level):
                        self.chain(level, t, j).wait_send()

            return 0

        lax.fori_loop(0, self.chunks, turn, 0)


def kernel(
    n, g, fs, chunks,
    q_hbm, k_hbm, v_hbm, c_hbm, gain_ref,
    qg, kg, vg, gg_ref,
    q, k, v, cot, do, att, kg_l, vg_l, w_top, w_low,
    own, slots, carry, fwd, before, outs, result,
    sq, cr, stats, gp, gz,
    in_sem, a_send, a_recv, z_send, z_recv, b_send, b_recv,
    f_send, f_recv, g_send, g_recv, h_send, h_recv,
):
    rows, width = q.shape
    heads = width // HEAD_DIM
    half = rows // 2
    m = n // g
    me = lax.axis_index("seq")
    mine = lax.axis_index("fsdp")
    z, i = me // g, lax.rem(me, g)

    loads = [
        pltpu.make_async_copy(src, dst, in_sem.at[at])
        for at, (src, dst) in enumerate(((k_hbm, k), (v_hbm, v), (q_hbm, q), (c_hbm, cot)))
    ]
    for load in loads:
        load.start()

    barrier = pltpu.get_barrier_semaphore()
    for d in range(1, g):
        pl.semaphore_signal(
            barrier, inc=1, device_id={"seq": z * g + lax.rem(i + d, g)}, device_id_type=MESH
        )
    for d in range(1, m):
        pl.semaphore_signal(
            barrier, inc=1, device_id={"seq": lax.rem(z + d, m) * g + i}, device_id_type=MESH
        )
    for d in range(1, fs):
        pl.semaphore_signal(
            barrier, inc=1, device_id={"fsdp": lax.rem(mine + d, fs)}, device_id_type=MESH
        )

    sems = (a_send, a_recv, z_send, z_recv, b_send, b_recv)
    scans = [
        Scan(w, w == 1, g, m, chunks, tuple(r.at[w] for r in (own, slots, carry, fwd, before, outs, result)), sems)
        for w in range(2)
    ]
    per = heads // g

    window = min(2, chunks)

    def make_states(scan, state_of, first, last, send):
        def turn(t, _):
            j, d = t // g, lax.rem(t + 1, g)
            p = scan.peer(d)
            state = state_of(p * per + j)
            scan.own[scan.rows(p, j)] = state

            @pl.when(d == 0)
            def _():
                scan.slots[i, scan.part(j)] = state

            if send:

                @pl.when(d != 0)
                def _():
                    scan.spread(d, j).start()

            return 0

        lax.fori_loop(first * g, last * g, turn, 0)

    def make_all(scan, state_of):
        for head in range(heads):
            scan.own[pl.ds(head * HEAD_DIM, HEAD_DIM)] = state_of(head)
        for j in range(chunks):
            scan.slots[i, scan.part(j)] = scan.own[scan.rows(i, j)]
            for d in range(1, g):
                scan.spread(d, j).start()

    def arrivals(scan, visit):
        def turn(t, _):
            j, d = t // g, lax.rem(t, g)

            @pl.when(d != 0)
            def _():
                scan.hand(d, j, True).wait_recv()

            visit(scan.peer(d) * per + j)
            return 0

        if per:
            lax.fori_loop(0, chunks * g, turn, 0)
        else:
            for j in range(chunks):
                for d in range(1, g):
                    scan.hand(d, j, True).wait_recv()
            for head in range(heads):
                visit(head)

    def state_at(scan, head):
        at = pl.ds(pl.multiple_of(head * HEAD_DIM, HEAD_DIM), HEAD_DIM)
        return scan.result[at].astype(BF16)

    loads[0].wait()
    loads[1].wait()
    pl.semaphore_wait(barrier, (g - 1) + (m - 1) + (fs - 1))

    def state(head):
        return dot_atb(k[:, cols_of(head)], v[:, cols_of(head)])

    if per:
        make_states(scans[0], state, 0, window, True)
        make_states(scans[0], state, window, chunks, False)
    else:
        make_all(scans[0], state)
    loads[2].wait()

    top, low = pl.ds(0, half), pl.ds(half, half)

    def inside(head):
        cols = cols_of(head)
        vh = v[:, cols]
        q0, q1, k0, k1 = q[top, cols], q[low, cols], k[top, cols], k[low, cols]
        w0 = lower(dot_abt(q0, k0))
        w1 = bottom(dot_abt(q1, k0), dot_abt(q1, k1))
        att[top, cols] = dot_ab(w0, v[top, cols])
        att[low, cols] = dot_ab(w1, vh)
        w_top[head] = top_of(dot_abt(k0, q0), dot_abt(k0, q1))
        w_low[head] = upper(dot_abt(k1, q1))

    def beside(scan, unit, width, start, sends):
        def turn(u, _):
            for at in range(width):
                unit(u * width + at)
            j = u + start
            if sends:

                @pl.when(j + window < chunks)
                def _():
                    scan.sent(j)
                    for d in range(1, g):
                        scan.spread(d, j + window).start()

            @pl.when(j < chunks)
            def _():
                scan.gather(j)
                scan.process(j)

            return 0

        if per and heads % width == 0:
            lax.fori_loop(0, heads // width, turn, 0)
        else:
            for head in range(heads):
                unit(head)
            for j in range(start, chunks):
                scan.gather(j)
                scan.process(j)

    beside(scans[0], inside, 2, 0, True)
    loads[3].wait()

    sq[...] = jnp.zeros_like(sq)
    cr[...] = jnp.zeros_like(cr)

    def finish(head):
        cols = cols_of(head)
        a = att[:, cols] + dot_ab(q[:, cols], state_at(scans[0], head))
        att[:, cols] = a
        sq[...] += a * a
        cr[...] += a * (cot[:, cols].astype(F32) * gain_ref[:, cols])

    arrivals(scans[0], finish)

    lane = lax.broadcasted_iota(jnp.int32, sq.shape, 1)
    stats[mine] = jnp.where(
        lane < HEAD_DIM // 2,
        jnp.sum(sq[...], axis=1, keepdims=True),
        jnp.sum(cr[...], axis=1, keepdims=True),
    )

    def share(d, slot):
        return pltpu.make_async_remote_copy(
            src_ref=stats.at[mine],
            dst_ref=stats.at[slot],
            send_sem=f_send.at[d],
            recv_sem=f_recv.at[slot],
            device_id={"fsdp": lax.rem(mine + d, fs)},
            device_id_type=MESH,
        )

    for d in range(1, fs):
        share(d, mine).start()
    for d in range(1, fs):
        share(d, lax.rem(mine + d, fs)).wait_recv()
    both = stats[0]
    for f in range(1, fs):
        both = both + stats[f]
    inv = lax.rsqrt(both[:, 0:1] / HD + EPS)
    mean = both[:, HEAD_DIM - 1 : HEAD_DIM] * inv / HD
    sq[...] = jnp.broadcast_to(inv, sq.shape)
    cr[...] = jnp.broadcast_to(mean, cr.shape)

    def grad_state(head):
        cols = cols_of(head)
        up = cot[:, cols].astype(F32)
        normed = att[:, cols] * sq[...]
        gp[i, :, cols] = jnp.sum(up * normed, axis=0, keepdims=True)
        d_h = ((up * gain_ref[:, cols] - normed * cr[...]) * sq[...]).astype(BF16)
        do[:, cols] = d_h
        return dot_atb(q[:, cols], d_h)

    def next_states(j, _):
        scans[1].sent(j - window)
        make_states(scans[1], grad_state, j, j + 1, True)
        scans[1].gather(j - window)
        scans[1].process(j - window)
        return 0

    if per:
        make_states(scans[1], grad_state, 0, window, True)
        lax.fori_loop(window, chunks, next_states, 0)
    else:
        make_all(scans[1], grad_state)

    def gain_near(d, slot):
        return pltpu.make_async_remote_copy(
            src_ref=gp.at[i],
            dst_ref=gp.at[slot],
            send_sem=g_send.at[d],
            recv_sem=g_recv.at[slot],
            device_id={"seq": z * g + lax.rem(i + d, g)},
            device_id_type=MESH,
        )

    def gain_far(d, slot):
        return pltpu.make_async_remote_copy(
            src_ref=gz.at[z],
            dst_ref=gz.at[slot],
            send_sem=h_send.at[d],
            recv_sem=h_recv.at[slot],
            device_id={"seq": lax.rem(z + d, m) * g + i},
            device_id_type=MESH,
        )

    for d in range(1, g):
        gain_near(d, i).start()

    def backward(head):
        cols = cols_of(head)
        qh, kh, dh = q[:, cols], k[:, cols], do[:, cols]
        q1, k0, v0, v1 = q[low, cols], k[top, cols], v[top, cols], v[low, cols]
        d0, d1 = do[top, cols], do[low, cols]
        from_prefix = dot_abt(dh, state_at(scans[0], head))
        s0 = lower(dot_abt(d0, v0))
        s1 = bottom(dot_abt(d1, v0), dot_abt(d1, v1))
        qg[top, cols] = (dot_ab(s0, k0) + from_prefix[:half]).astype(BF16)
        qg[low, cols] = (dot_ab(s1, kh) + from_prefix[half:]).astype(BF16)
        t0 = top_of(dot_abt(v0, d0), dot_abt(v0, d1))
        t1 = upper(dot_abt(v1, d1))
        kg_l[top, cols] = dot_ab(t0, qh)
        kg_l[low, cols] = dot_ab(t1, q1)
        vg_l[top, cols] = dot_ab(w_top[head], dh)
        vg_l[low, cols] = dot_ab(w_low[head], d1)

    beside(scans[1], backward, 2, chunks - window if per else 0, False)

    for d in range(1, g):
        gain_near(d, lax.rem(i + d, g)).wait_recv()
    near = gp[0]
    for p in range(1, g):
        near = near + gp[p]
    gz[z] = near
    for d in range(1, m):
        gain_far(d, z).start()

    def last(head):
        cols = cols_of(head)
        suffix = state_at(scans[1], head)
        kg[:, cols] = (kg_l[:, cols] + dot_abt(v[:, cols], suffix)).astype(BF16)
        vg[:, cols] = (vg_l[:, cols] + dot_ab(k[:, cols], suffix)).astype(BF16)

    arrivals(scans[1], last)

    for d in range(1, m):
        gain_far(d, lax.rem(z + d, m)).wait_recv()
    total = gz[0]
    for p in range(1, m):
        total = total + gz[p]
    gg_ref[...] = total * (1.0 / math.sqrt(rows * n))

    for scan in scans:
        scan.drain(window)
    for d in range(1, fs):
        share(d, mine).wait_send()
    for d in range(1, g):
        gain_near(d, i).wait_send()
    for d in range(1, m):
        gain_far(d, z).wait_send()


def store(qg, kg, vg, gg, qg_hbm, kg_hbm, vg_hbm, gg_hbm, sem):
    copies = [
        pltpu.make_async_copy(src, dst, sem.at[at])
        for at, (src, dst) in enumerate(((qg, qg_hbm), (kg, kg_hbm), (vg, vg_hbm), (gg, gg_hbm)))
    ]
    for copy in copies:
        copy.start()
    for copy in copies:
        copy.wait()


def solution(mesh):
    n, fs = mesh.shape["seq"], mesh.shape["fsdp"]
    g = group_size(n)
    m = n // g

    def shards(query, key, value, cotangent, gain):
        rows, width = query.shape
        heads = width // HEAD_DIM
        chunks = max(heads // g, 1)
        state = heads * HEAD_DIM
        piece = state // g
        levels = max(m.bit_length() - 1, 1)
        any_space = pl.BlockSpec(memory_space=pl.ANY)
        vmem = pl.BlockSpec(memory_space=pltpu.VMEM)
        dma = pltpu.SemaphoreType.DMA
        big, small = jax.ShapeDtypeStruct((rows, width), BF16), jax.ShapeDtypeStruct((1, width), F32)
        held = pltpu.VMEM((rows, width), BF16)
        products = 6 * rows * rows + 6 * rows * HEAD_DIM
        results = pl.pallas_call(
            functools.partial(kernel, n, g, fs, chunks),
            out_shape=(held, held, held, pltpu.VMEM((1, width), F32)),
            in_specs=[any_space] * 4 + [vmem],
            out_specs=(vmem, vmem, vmem, vmem),
            scratch_shapes=[pltpu.VMEM((rows, width), BF16)] * 5
            + [pltpu.VMEM((rows, width), F32)] * 3
            + [
                pltpu.VMEM((heads, rows // 2, rows), BF16),
                pltpu.VMEM((heads, rows // 2, rows // 2), BF16),
                pltpu.VMEM((2, state, HEAD_DIM), F32),
                pltpu.VMEM((2, g, piece, HEAD_DIM), F32),
                pltpu.VMEM((2, levels, piece, HEAD_DIM), F32),
                pltpu.VMEM((2, levels, piece, HEAD_DIM), F32),
                pltpu.VMEM((2, piece, HEAD_DIM), F32),
                pltpu.VMEM((2, g, piece, HEAD_DIM), F32),
                pltpu.VMEM((2, state, HEAD_DIM), F32),
                pltpu.VMEM((rows, HEAD_DIM), F32),
                pltpu.VMEM((rows, HEAD_DIM), F32),
                pltpu.VMEM((fs, rows, HEAD_DIM), F32),
                pltpu.VMEM((g, 1, width), F32),
                pltpu.VMEM((m, 1, width), F32),
                dma((4,)),
                dma((2, g, chunks)),
                dma((2, g, chunks)),
                dma((2, levels, max(m // 2, 1), chunks)),
                dma((2, levels, chunks)),
                dma((2, g, chunks)),
                dma((2, g, chunks)),
                dma((fs,)),
                dma((fs,)),
                dma((g,)),
                dma((g,)),
                dma((m,)),
                dma((m,)),
            ],
            compiler_params=pltpu.CompilerParams(
                collective_id=0, has_side_effects=True, vmem_limit_bytes=50 * 2**20
            ),
            cost_estimate=pl.CostEstimate(
                flops=2 * products * width, bytes_accessed=14 * rows * width, transcendentals=rows
            ),
        )(query, key, value, cotangent, gain.reshape(1, width))
        grads = pl.pallas_call(
            store,
            out_shape=(big, big, big, small),
            in_specs=[any_space] * 4,
            out_specs=(any_space,) * 4,
            scratch_shapes=[dma((4,))],
            compiler_params=pltpu.CompilerParams(vmem_limit_bytes=2**20),
        )(*results)
        return (*grads[:3], grads[3].reshape(width))

    in_specs = (P("seq", "fsdp"), P("seq", "fsdp"), P("seq", "fsdp"), P("seq", "fsdp"), P("fsdp"))
    out_specs = (P("seq", "fsdp"), P("seq", "fsdp"), P("seq", "fsdp"), P("fsdp"))
    return jax.shard_map(shards, mesh=mesh, in_specs=in_specs, out_specs=out_specs, check_vma=False)
```

```python
import functools
import math

import jax
import jax.numpy as jnp
from jax import lax
from jax.experimental import pallas as pl
from jax.experimental.pallas import tpu as pltpu
from jax.sharding import PartitionSpec as P

HEAD_DIM = 128
HD = 4096
EPS = 1e-05
MESH = pl.DeviceIdType.MESH
F32 = jnp.float32
BF16 = jnp.bfloat16


def dot_ab(a, b):
    return lax.dot_general(a, b, (((1,), (0,)), ((), ())), preferred_element_type=F32)


def dot_abt(a, b):
    return lax.dot_general(a, b, (((1,), (1,)), ((), ())), preferred_element_type=F32)


def dot_atb(a, b):
    return lax.dot_general(a, b, (((0,), (0,)), ((), ())), preferred_element_type=F32)


def group_size(count):
    size = 1
    while size * size < count:
        size *= 2
    return size


def lower(block, offset):
    row = lax.broadcasted_iota(jnp.int32, block.shape, 0) + offset
    col = lax.broadcasted_iota(jnp.int32, block.shape, 1)
    return jnp.where(row >= col, block, 0.0).astype(BF16)


def upper(block):
    row = lax.broadcasted_iota(jnp.int32, block.shape, 0)
    col = lax.broadcasted_iota(jnp.int32, block.shape, 1)
    return jnp.where(row <= col, block, 0.0).astype(BF16)


def cols_of(head):
    return pl.ds(pl.multiple_of(head * HEAD_DIM, HEAD_DIM), HEAD_DIM)


class Scan:
    def __init__(self, which, reverse, g, m, chunks, refs, sems):
        self.which, self.reverse, self.g, self.m, self.chunks = which, reverse, g, m, chunks
        self.own, self.slots, self.carry, self.fwd, self.before, self.outs, self.result = refs
        self.a_send, self.a_recv, self.z_send, self.z_recv, self.b_send, self.b_recv = sems
        me = lax.axis_index("seq")
        self.z, self.i = me // g, lax.rem(me, g)
        self.piece = self.own.shape[0] // g
        self.ch = self.piece // chunks

    def peer(self, d):
        peer, bit = 0, 1
        while bit < self.g:
            peer = peer + lax.rem(self.i // bit + d // bit, 2) * bit
            bit *= 2
        return peer

    def rows(self, p, j):
        return pl.ds(pl.multiple_of(p * self.piece + j * self.ch, self.ch), self.ch)

    def part(self, j):
        return pl.ds(pl.multiple_of(j * self.ch, self.ch), self.ch)

    def spread(self, d, j, arriving=False):
        p = self.peer(d)
        slot = p if arriving else self.i
        return pltpu.make_async_remote_copy(
            src_ref=self.own.at[self.rows(p, j)],
            dst_ref=self.slots.at[slot, self.part(j)],
            send_sem=self.a_send.at[self.which, d, j],
            recv_sem=self.a_recv.at[self.which, slot, j],
            device_id={"seq": self.z * self.g + p},
            device_id_type=MESH,
        )

    def place(self):
        return self.m - 1 - self.z if self.reverse else self.z

    def chain(self, level, t, j):
        place = jnp.clip(self.place() + 1 + t, 0, self.m - 1)
        group = self.m - 1 - place if self.reverse else place
        return pltpu.make_async_remote_copy(
            src_ref=self.fwd.at[level, self.part(j)],
            dst_ref=self.carry.at[level, self.part(j)],
            send_sem=self.z_send.at[self.which, level, t, j],
            recv_sem=self.z_recv.at[self.which, level, j],
            device_id={"seq": group * self.g + self.i},
            device_id_type=MESH,
        )

    def levels(self):
        return range(self.m.bit_length() - 1)

    def sends(self, level):
        return lax.rem(self.place(), 2 << level) == (1 << level) - 1

    def receives(self, level):
        return lax.rem(self.place(), 2 << level) >= 1 << level

    def forward(self, level, j, value):
        @pl.when(self.sends(level))
        def _():
            self.fwd[level, self.part(j)] = value()
            for t in range(1 << level):
                self.chain(level, t, j).start()

    def hand(self, d, j, arriving=False):
        p = self.peer(d)
        owner = p if arriving else self.i
        return pltpu.make_async_remote_copy(
            src_ref=self.outs.at[p, self.part(j)],
            dst_ref=self.result.at[self.rows(owner, j)],
            send_sem=self.b_send.at[self.which, d, j],
            recv_sem=self.b_recv.at[self.which, owner, j],
            device_id={"seq": self.z * self.g + p},
            device_id_type=MESH,
        )

    def total(self, j):
        total = self.slots[0, self.part(j)]
        for p in range(1, self.g):
            total = total + self.slots[p, self.part(j)]
        return total

    def gather(self, j):
        for d in range(1, self.g):
            self.spread(d, j, True).wait_recv()
        if self.m > 1:
            self.forward(0, j, lambda: self.total(j))

    def process(self, j):
        part = self.part(j)
        self.before[part] = jnp.zeros((self.ch, HEAD_DIM), F32)
        for level in self.levels():
            if level:
                self.forward(level, j, lambda: self.before[part] + self.total(j))

            @pl.when(self.receives(level))
            def _():
                self.chain(level, 0, j).wait_recv()
                self.before[part] += self.carry[level, part]

        running = self.before[part]
        order = range(self.g)
        for p in reversed(order) if self.reverse else order:
            self.outs[p, part] = running
            running = running + self.slots[p, part]
        for d in reversed(range(1, self.g)):
            self.hand(d, j).start()
        self.result[self.rows(self.i, j)] = self.outs[self.i, part]

    def drain(self):
        def turn(j, _):
            for d in range(1, self.g):
                self.spread(d, j).wait_send()
                self.hand(d, j).wait_send()
            for level in self.levels():

                @pl.when(self.sends(level))
                def _():
                    for t in range(1 << level):
                        self.chain(level, t, j).wait_send()

            return 0

        lax.fori_loop(0, self.chunks, turn, 0)


def kernel(
    n, g, fs, chunks,
    q_hbm, k_hbm, v_hbm, c_hbm, gain_ref,
    qg, kg, vg, gg_ref,
    q, k, v, cot, do, att, kg_l, vg_l, w_top, w_low,
    own, slots, carry, fwd, before, outs, result,
    sq, cr, stats, gp, gz,
    in_sem, head_sem, a_send, a_recv, z_send, z_recv, b_send, b_recv,
    f_send, f_recv, g_send, g_recv, h_send, h_recv,
):
    rows, width = q.shape
    heads = width // HEAD_DIM
    half = rows // 2
    m = n // g
    me = lax.axis_index("seq")
    mine = lax.axis_index("fsdp")
    z, i = me // g, lax.rem(me, g)

    def load_head(at, head):
        src, dst = ((k_hbm, k), (v_hbm, v))[at]
        cols = cols_of(head)
        return pltpu.make_async_copy(src.at[:, cols], dst.at[:, cols], head_sem.at[at, head])

    loads = [
        pltpu.make_async_copy(src, dst, in_sem.at[at])
        for at, (src, dst) in enumerate(((q_hbm, q), (c_hbm, cot)))
    ]

    barrier = pltpu.get_barrier_semaphore()
    for d in range(1, g):
        pl.semaphore_signal(
            barrier, inc=1, device_id={"seq": z * g + lax.rem(i + d, g)}, device_id_type=MESH
        )
    for d in range(1, m):
        pl.semaphore_signal(
            barrier, inc=1, device_id={"seq": lax.rem(z + d, m) * g + i}, device_id_type=MESH
        )
    for d in range(1, fs):
        pl.semaphore_signal(
            barrier, inc=1, device_id={"fsdp": lax.rem(mine + d, fs)}, device_id_type=MESH
        )

    sems = (a_send, a_recv, z_send, z_recv, b_send, b_recv)
    scans = [
        Scan(w, w == 1, g, m, chunks, tuple(r.at[w] for r in (own, slots, carry, fwd, before, outs, result)), sems)
        for w in range(2)
    ]
    per = heads // g

    def make_states(scan, state_of):
        def turn(t, _):
            j, d = t // g, g - 1 - lax.rem(t, g)
            p = scan.peer(d)
            state = state_of(p * per + j)
            scan.own[scan.rows(p, j)] = state

            @pl.when(d == 0)
            def _():
                scan.slots[i, scan.part(j)] = state

            @pl.when(d != 0)
            def _():
                scan.spread(d, j).start()

            return 0

        if per:
            lax.fori_loop(0, chunks * g, turn, 0)
        else:
            for head in range(heads):
                scan.own[pl.ds(head * HEAD_DIM, HEAD_DIM)] = state_of(head)
            for j in range(chunks):
                scan.slots[i, scan.part(j)] = scan.own[scan.rows(i, j)]
                for d in range(1, g):
                    scan.spread(d, j).start()

    def arrivals(scan, visit):
        def turn(t, _):
            j, d = t // g, lax.rem(t, g)

            @pl.when(d != 0)
            def _():
                scan.hand(d, j, True).wait_recv()

            visit(scan.peer(d) * per + j)
            return 0

        if per:
            lax.fori_loop(0, chunks * g, turn, 0)
        else:
            for j in range(chunks):
                for d in range(1, g):
                    scan.hand(d, j, True).wait_recv()
            for head in range(heads):
                visit(head)

    def state_at(scan, head):
        at = pl.ds(pl.multiple_of(head * HEAD_DIM, HEAD_DIM), HEAD_DIM)
        return scan.result[at].astype(BF16)

    def begin(t, _):
        head = scans[0].peer(g - 1 - lax.rem(t, g)) * per + t // g if per else t
        load_head(0, head).start()
        load_head(1, head).start()
        return 0

    lax.fori_loop(0, heads, begin, 0)
    for load in loads:
        load.start()
    pl.semaphore_wait(barrier, (g - 1) + (m - 1) + (fs - 1))

    def state(head):
        load_head(0, head).wait()
        load_head(1, head).wait()
        return dot_atb(k[:, cols_of(head)], v[:, cols_of(head)])

    make_states(scans[0], state)
    loads[0].wait()

    top, low = pl.ds(0, half), pl.ds(half, half)

    def inside(head):
        cols = cols_of(head)
        kh, vh = k[:, cols], v[:, cols]
        w0 = lower(dot_abt(q[top, cols], k[top, cols]), 0)
        w1 = lower(dot_abt(q[low, cols], kh), half)
        att[top, cols] = dot_ab(w0, v[top, cols])
        att[low, cols] = dot_ab(w1, vh)
        w_top[head] = upper(dot_abt(k[top, cols], q[:, cols]))
        w_low[head] = upper(dot_abt(k[low, cols], q[low, cols]))

    def beside(scan, unit, ahead, between):
        step = ahead + between

        def turn(u, _):
            unit(u)
            j = u // step

            @pl.when(jnp.logical_and(lax.rem(u, step) == ahead - 1, j < chunks))
            def _():
                scan.gather(j)

            @pl.when(jnp.logical_and(lax.rem(u, step) == step - 1, j < chunks))
            def _():
                scan.process(j)

            return 0

        if heads >= step * chunks:
            lax.fori_loop(0, heads, turn, 0)
        else:
            for head in range(heads):
                unit(head)
            for j in range(chunks):
                scan.gather(j)
                scan.process(j)

    beside(scans[0], inside, 2, 1)
    loads[1].wait()

    sq[...] = jnp.zeros_like(sq)
    cr[...] = jnp.zeros_like(cr)

    def finish(head):
        cols = cols_of(head)
        a = att[:, cols] + dot_ab(q[:, cols], state_at(scans[0], head))
        att[:, cols] = a
        sq[...] += a * a
        cr[...] += a * (cot[:, cols].astype(F32) * gain_ref[:, cols])

    arrivals(scans[0], finish)

    lane = lax.broadcasted_iota(jnp.int32, sq.shape, 1)
    stats[mine] = jnp.where(
        lane < HEAD_DIM // 2,
        jnp.sum(sq[...], axis=1, keepdims=True),
        jnp.sum(cr[...], axis=1, keepdims=True),
    )

    def share(d, slot):
        return pltpu.make_async_remote_copy(
            src_ref=stats.at[mine],
            dst_ref=stats.at[slot],
            send_sem=f_send.at[d],
            recv_sem=f_recv.at[slot],
            device_id={"fsdp": lax.rem(mine + d, fs)},
            device_id_type=MESH,
        )

    for d in range(1, fs):
        share(d, mine).start()
    for d in range(1, fs):
        share(d, lax.rem(mine + d, fs)).wait_recv()
    both = stats[0]
    for f in range(1, fs):
        both = both + stats[f]
    inv = lax.rsqrt(both[:, 0:1] / HD + EPS)
    mean = both[:, HEAD_DIM - 1 : HEAD_DIM] * inv / HD
    sq[...] = jnp.broadcast_to(inv, sq.shape)
    cr[...] = jnp.broadcast_to(mean, cr.shape)

    def grad_state(head):
        cols = cols_of(head)
        up = cot[:, cols].astype(F32)
        normed = att[:, cols] * sq[...]
        gp[i, :, cols] = jnp.sum(up * normed, axis=0, keepdims=True)
        d_h = ((up * gain_ref[:, cols] - normed * cr[...]) * sq[...]).astype(BF16)
        do[:, cols] = d_h
        return dot_atb(q[:, cols], d_h)

    make_states(scans[1], grad_state)

    def gain_near(d, slot):
        return pltpu.make_async_remote_copy(
            src_ref=gp.at[i],
            dst_ref=gp.at[slot],
            send_sem=g_send.at[d],
            recv_sem=g_recv.at[slot],
            device_id={"seq": z * g + lax.rem(i + d, g)},
            device_id_type=MESH,
        )

    def gain_far(d, slot):
        return pltpu.make_async_remote_copy(
            src_ref=gz.at[z],
            dst_ref=gz.at[slot],
            send_sem=h_send.at[d],
            recv_sem=h_recv.at[slot],
            device_id={"seq": lax.rem(z + d, m) * g + i},
            device_id_type=MESH,
        )

    for d in range(1, g):
        gain_near(d, i).start()

    def backward(head):
        cols = cols_of(head)
        qh, kh, vh, dh = q[:, cols], k[:, cols], v[:, cols], do[:, cols]
        q1, k0, v0, d1 = q[low, cols], k[top, cols], v[top, cols], do[low, cols]
        from_prefix = dot_abt(dh, state_at(scans[0], head))
        s0 = lower(dot_abt(do[top, cols], v0), 0)
        s1 = lower(dot_abt(d1, vh), half)
        qg[top, cols] = (dot_ab(s0, k0) + from_prefix[:half]).astype(BF16)
        qg[low, cols] = (dot_ab(s1, kh) + from_prefix[half:]).astype(BF16)
        t0 = upper(dot_abt(v0, dh))
        t1 = upper(dot_abt(v[low, cols], d1))
        kg_l[top, cols] = dot_ab(t0, qh)
        kg_l[low, cols] = dot_ab(t1, q1)
        vg_l[top, cols] = dot_ab(w_top[head], dh)
        vg_l[low, cols] = dot_ab(w_low[head], d1)

    beside(scans[1], backward, 1, 1)

    for d in range(1, g):
        gain_near(d, lax.rem(i + d, g)).wait_recv()
    near = gp[0]
    for p in range(1, g):
        near = near + gp[p]
    gz[z] = near
    for d in range(1, m):
        gain_far(d, z).start()

    def last(head):
        cols = cols_of(head)
        suffix = state_at(scans[1], head)
        kg[:, cols] = (kg_l[:, cols] + dot_abt(v[:, cols], suffix)).astype(BF16)
        vg[:, cols] = (vg_l[:, cols] + dot_ab(k[:, cols], suffix)).astype(BF16)

    arrivals(scans[1], last)

    for d in range(1, m):
        gain_far(d, lax.rem(z + d, m)).wait_recv()
    total = gz[0]
    for p in range(1, m):
        total = total + gz[p]
    gg_ref[...] = total * (1.0 / math.sqrt(rows * n))

    for scan in scans:
        scan.drain()
    for d in range(1, fs):
        share(d, mine).wait_send()
    for d in range(1, g):
        gain_near(d, i).wait_send()
    for d in range(1, m):
        gain_far(d, z).wait_send()


def store(qg, kg, vg, gg, qg_hbm, kg_hbm, vg_hbm, gg_hbm, sem):
    copies = [
        pltpu.make_async_copy(src, dst, sem.at[at])
        for at, (src, dst) in enumerate(((qg, qg_hbm), (kg, kg_hbm), (vg, vg_hbm), (gg, gg_hbm)))
    ]
    for copy in copies:
        copy.start()
    for copy in copies:
        copy.wait()


def solution(mesh):
    n, fs = mesh.shape["seq"], mesh.shape["fsdp"]
    g = group_size(n)
    m = n // g

    def shards(query, key, value, cotangent, gain):
        rows, width = query.shape
        heads = width // HEAD_DIM
        chunks = max(heads // g, 1)
        state = heads * HEAD_DIM
        piece = state // g
        levels = max(m.bit_length() - 1, 1)
        any_space = pl.BlockSpec(memory_space=pl.ANY)
        vmem = pl.BlockSpec(memory_space=pltpu.VMEM)
        dma = pltpu.SemaphoreType.DMA
        big, small = jax.ShapeDtypeStruct((rows, width), BF16), jax.ShapeDtypeStruct((1, width), F32)
        held = pltpu.VMEM((rows, width), BF16)
        products = 6 * rows * rows + 6 * rows * HEAD_DIM
        results = pl.pallas_call(
            functools.partial(kernel, n, g, fs, chunks),
            out_shape=(held, held, held, pltpu.VMEM((1, width), F32)),
            in_specs=[any_space] * 4 + [vmem],
            out_specs=(vmem, vmem, vmem, vmem),
            scratch_shapes=[pltpu.VMEM((rows, width), BF16)] * 5
            + [pltpu.VMEM((rows, width), F32)] * 3
            + [
                pltpu.VMEM((heads, rows // 2, rows), BF16),
                pltpu.VMEM((heads, rows // 2, rows // 2), BF16),
                pltpu.VMEM((2, state, HEAD_DIM), F32),
                pltpu.VMEM((2, g, piece, HEAD_DIM), F32),
                pltpu.VMEM((2, levels, piece, HEAD_DIM), F32),
                pltpu.VMEM((2, levels, piece, HEAD_DIM), F32),
                pltpu.VMEM((2, piece, HEAD_DIM), F32),
                pltpu.VMEM((2, g, piece, HEAD_DIM), F32),
                pltpu.VMEM((2, state, HEAD_DIM), F32),
                pltpu.VMEM((rows, HEAD_DIM), F32),
                pltpu.VMEM((rows, HEAD_DIM), F32),
                pltpu.VMEM((fs, rows, HEAD_DIM), F32),
                pltpu.VMEM((g, 1, width), F32),
                pltpu.VMEM((m, 1, width), F32),
                dma((2,)),
                dma((2, heads)),
                dma((2, g, chunks)),
                dma((2, g, chunks)),
                dma((2, levels, max(m // 2, 1), chunks)),
                dma((2, levels, chunks)),
                dma((2, g, chunks)),
                dma((2, g, chunks)),
                dma((fs,)),
                dma((fs,)),
                dma((g,)),
                dma((g,)),
                dma((m,)),
                dma((m,)),
            ],
            compiler_params=pltpu.CompilerParams(
                collective_id=0, has_side_effects=True, vmem_limit_bytes=50 * 2**20
            ),
            cost_estimate=pl.CostEstimate(
                flops=2 * products * width, bytes_accessed=14 * rows * width, transcendentals=rows
            ),
        )(query, key, value, cotangent, gain.reshape(1, width))
        grads = pl.pallas_call(
            store,
            out_shape=(big, big, big, small),
            in_specs=[any_space] * 4,
            out_specs=(any_space,) * 4,
            scratch_shapes=[dma((4,))],
            compiler_params=pltpu.CompilerParams(vmem_limit_bytes=2**20),
        )(*results)
        return (*grads[:3], grads[3].reshape(width))

    in_specs = (P("seq", "fsdp"), P("seq", "fsdp"), P("seq", "fsdp"), P("seq", "fsdp"), P("fsdp"))
    out_specs = (P("seq", "fsdp"), P("seq", "fsdp"), P("seq", "fsdp"), P("fsdp"))
    return jax.shard_map(shards, mesh=mesh, in_specs=in_specs, out_specs=out_specs, check_vma=False)
```

```python
import functools
import math

import jax
import jax.numpy as jnp
from jax import lax
from jax.experimental import pallas as pl
from jax.experimental.pallas import tpu as pltpu
from jax.sharding import PartitionSpec as P

HEAD_DIM = 128
HD = 4096
EPS = 1e-05
MESH = pl.DeviceIdType.MESH
F32 = jnp.float32
BF16 = jnp.bfloat16


def dot_ab(a, b):
    return lax.dot_general(a, b, (((1,), (0,)), ((), ())), preferred_element_type=F32)


def dot_abt(a, b):
    return lax.dot_general(a, b, (((1,), (1,)), ((), ())), preferred_element_type=F32)


def dot_atb(a, b):
    return lax.dot_general(a, b, (((0,), (0,)), ((), ())), preferred_element_type=F32)


def group_size(count):
    size = 1
    while size * size < count:
        size *= 2
    return size


def lower(block, offset):
    row = lax.broadcasted_iota(jnp.int32, block.shape, 0) + offset
    col = lax.broadcasted_iota(jnp.int32, block.shape, 1)
    return jnp.where(row >= col, block, 0.0).astype(BF16)


def upper(block):
    row = lax.broadcasted_iota(jnp.int32, block.shape, 0)
    col = lax.broadcasted_iota(jnp.int32, block.shape, 1)
    return jnp.where(row <= col, block, 0.0).astype(BF16)


def cols_of(head):
    return pl.ds(pl.multiple_of(head * HEAD_DIM, HEAD_DIM), HEAD_DIM)


class Scan:
    def __init__(self, which, reverse, g, m, chunks, refs, sems):
        self.which, self.reverse, self.g, self.m, self.chunks = which, reverse, g, m, chunks
        self.own, self.slots, self.carry, self.fwd, self.before, self.outs, self.result = refs
        self.a_send, self.a_recv, self.z_send, self.z_recv, self.b_send, self.b_recv = sems
        me = lax.axis_index("seq")
        self.z, self.i = me // g, lax.rem(me, g)
        self.piece = self.own.shape[0] // g
        self.ch = self.piece // chunks

    def peer(self, d):
        return lax.rem(self.i + d, self.g)

    def rows(self, p, j):
        return pl.ds(pl.multiple_of(p * self.piece + j * self.ch, self.ch), self.ch)

    def part(self, j):
        return pl.ds(pl.multiple_of(j * self.ch, self.ch), self.ch)

    def spread(self, d, j, arriving=False):
        p = self.peer(d)
        slot = p if arriving else self.i
        return pltpu.make_async_remote_copy(
            src_ref=self.own.at[self.rows(p, j)],
            dst_ref=self.slots.at[slot, self.part(j)],
            send_sem=self.a_send.at[self.which, d, j],
            recv_sem=self.a_recv.at[self.which, slot, j],
            device_id={"seq": self.z * self.g + p},
            device_id_type=MESH,
        )

    def place(self):
        return self.m - 1 - self.z if self.reverse else self.z

    def chain(self, level, t, j):
        place = jnp.clip(self.place() + 1 + t, 0, self.m - 1)
        group = self.m - 1 - place if self.reverse else place
        return pltpu.make_async_remote_copy(
            src_ref=self.fwd.at[level, self.part(j)],
            dst_ref=self.carry.at[level, self.part(j)],
            send_sem=self.z_send.at[self.which, level, t, j],
            recv_sem=self.z_recv.at[self.which, level, j],
            device_id={"seq": group * self.g + self.i},
            device_id_type=MESH,
        )

    def levels(self):
        return range(self.m.bit_length() - 1)

    def sends(self, level):
        return lax.rem(self.place(), 2 << level) == (1 << level) - 1

    def receives(self, level):
        return lax.rem(self.place(), 2 << level) >= 1 << level

    def forward(self, level, j, value):
        @pl.when(self.sends(level))
        def _():
            self.fwd[level, self.part(j)] = value()
            for t in range(1 << level):
                self.chain(level, t, j).start()

    def hand(self, d, j, arriving=False):
        p = self.peer(d)
        owner = p if arriving else self.i
        return pltpu.make_async_remote_copy(
            src_ref=self.outs.at[p, self.part(j)],
            dst_ref=self.result.at[self.rows(owner, j)],
            send_sem=self.b_send.at[self.which, d, j],
            recv_sem=self.b_recv.at[self.which, owner, j],
            device_id={"seq": self.z * self.g + p},
            device_id_type=MESH,
        )

    def total(self, j):
        total = self.slots[0, self.part(j)]
        for p in range(1, self.g):
            total = total + self.slots[p, self.part(j)]
        return total

    def gather(self, j):
        for d in range(1, self.g):
            self.spread(d, j, True).wait_recv()
        if self.m > 1:
            self.forward(0, j, lambda: self.total(j))

    def process(self, j):
        part = self.part(j)
        self.before[part] = jnp.zeros((self.ch, HEAD_DIM), F32)
        for level in self.levels():
            if level:
                self.forward(level, j, lambda: self.before[part] + self.total(j))

            @pl.when(self.receives(level))
            def _():
                self.chain(level, 0, j).wait_recv()
                self.before[part] += self.carry[level, part]

        running = self.before[part]
        order = range(self.g)
        for p in reversed(order) if self.reverse else order:
            self.outs[p, part] = running
            running = running + self.slots[p, part]
        for d in range(1, self.g):
            self.hand(d, j).start()
        self.result[self.rows(self.i, j)] = self.outs[self.i, part]

    def drain(self):
        def turn(j, _):
            for d in range(1, self.g):
                self.spread(d, j).wait_send()
                self.hand(d, j).wait_send()
            for level in self.levels():

                @pl.when(self.sends(level))
                def _():
                    for t in range(1 << level):
                        self.chain(level, t, j).wait_send()

            return 0

        lax.fori_loop(0, self.chunks, turn, 0)


def kernel(
    n, g, fs, chunks,
    q_hbm, k_hbm, v_hbm, c_hbm, gain_ref,
    qg, kg, vg, gg_ref,
    q, k, v, cot, do, att, kg_l, vg_l, w_top, w_low,
    own, slots, carry, fwd, before, outs, result,
    sq, cr, stats, gp, gz,
    in_sem, a_send, a_recv, z_send, z_recv, b_send, b_recv,
    f_send, f_recv, g_send, g_recv, h_send, h_recv,
):
    rows, width = q.shape
    heads = width // HEAD_DIM
    half = rows // 2
    m = n // g
    me = lax.axis_index("seq")
    mine = lax.axis_index("fsdp")
    z, i = me // g, lax.rem(me, g)

    loads = [
        pltpu.make_async_copy(src, dst, in_sem.at[at])
        for at, (src, dst) in enumerate(((k_hbm, k), (v_hbm, v), (q_hbm, q), (c_hbm, cot)))
    ]
    for load in loads:
        load.start()

    barrier = pltpu.get_barrier_semaphore()
    for d in range(1, g):
        pl.semaphore_signal(
            barrier, inc=1, device_id={"seq": z * g + lax.rem(i + d, g)}, device_id_type=MESH
        )
    for d in range(1, m):
        pl.semaphore_signal(
            barrier, inc=1, device_id={"seq": lax.rem(z + d, m) * g + i}, device_id_type=MESH
        )
    for d in range(1, fs):
        pl.semaphore_signal(
            barrier, inc=1, device_id={"fsdp": lax.rem(mine + d, fs)}, device_id_type=MESH
        )

    sems = (a_send, a_recv, z_send, z_recv, b_send, b_recv)
    scans = [
        Scan(w, w == 1, g, m, chunks, tuple(r.at[w] for r in (own, slots, carry, fwd, before, outs, result)), sems)
        for w in range(2)
    ]
    per = heads // g

    def make_states(scan, state_of):
        def turn(t, _):
            j, d = t // g, lax.rem(t + 1, g)
            p = scan.peer(d)
            state = state_of(p * per + j)
            scan.own[scan.rows(p, j)] = state

            @pl.when(d == 0)
            def _():
                scan.slots[i, scan.part(j)] = state

            @pl.when(d != 0)
            def _():
                scan.spread(d, j).start()

            return 0

        if per:
            lax.fori_loop(0, chunks * g, turn, 0)
        else:
            for head in range(heads):
                scan.own[pl.ds(head * HEAD_DIM, HEAD_DIM)] = state_of(head)
            for j in range(chunks):
                scan.slots[i, scan.part(j)] = scan.own[scan.rows(i, j)]
                for d in range(1, g):
                    scan.spread(d, j).start()

    def arrivals(scan, visit):
        def turn(t, _):
            j, d = t // g, lax.rem(t, g)

            @pl.when(d != 0)
            def _():
                scan.hand(d, j, True).wait_recv()

            visit(scan.peer(d) * per + j)
            return 0

        if per:
            lax.fori_loop(0, chunks * g, turn, 0)
        else:
            for j in range(chunks):
                for d in range(1, g):
                    scan.hand(d, j, True).wait_recv()
            for head in range(heads):
                visit(head)

    def state_at(scan, head):
        at = pl.ds(pl.multiple_of(head * HEAD_DIM, HEAD_DIM), HEAD_DIM)
        return scan.result[at].astype(BF16)

    loads[0].wait()
    loads[1].wait()
    pl.semaphore_wait(barrier, (g - 1) + (m - 1) + (fs - 1))
    make_states(scans[0], lambda head: dot_atb(k[:, cols_of(head)], v[:, cols_of(head)]))
    loads[2].wait()

    top, low = pl.ds(0, half), pl.ds(half, half)

    def inside(head):
        cols = cols_of(head)
        kh, vh = k[:, cols], v[:, cols]
        w0 = lower(dot_abt(q[top, cols], k[top, cols]), 0)
        w1 = lower(dot_abt(q[low, cols], kh), half)
        att[top, cols] = dot_ab(w0, v[top, cols])
        att[low, cols] = dot_ab(w1, vh)
        w_top[head] = upper(dot_abt(k[top, cols], q[:, cols]))
        w_low[head] = upper(dot_abt(k[low, cols], q[low, cols]))

    def beside(scan, unit, ahead, between):
        step = ahead + between

        def turn(u, _):
            unit(u)
            j = u // step

            @pl.when(jnp.logical_and(lax.rem(u, step) == ahead - 1, j < chunks))
            def _():
                scan.gather(j)

            @pl.when(jnp.logical_and(lax.rem(u, step) == step - 1, j < chunks))
            def _():
                scan.process(j)

            return 0

        if heads >= step * chunks:
            lax.fori_loop(0, heads, turn, 0)
        else:
            for head in range(heads):
                unit(head)
            for j in range(chunks):
                scan.gather(j)
                scan.process(j)

    beside(scans[0], inside, 2, 2)
    loads[3].wait()

    sq[...] = jnp.zeros_like(sq)
    cr[...] = jnp.zeros_like(cr)

    def finish(head):
        cols = cols_of(head)
        a = att[:, cols] + dot_ab(q[:, cols], state_at(scans[0], head))
        att[:, cols] = a
        sq[...] += a * a
        cr[...] += a * (cot[:, cols].astype(F32) * gain_ref[:, cols])

    arrivals(scans[0], finish)

    lane = lax.broadcasted_iota(jnp.int32, sq.shape, 1)
    stats[mine] = jnp.where(
        lane < HEAD_DIM // 2,
        jnp.sum(sq[...], axis=1, keepdims=True),
        jnp.sum(cr[...], axis=1, keepdims=True),
    )

    def share(d, slot):
        return pltpu.make_async_remote_copy(
            src_ref=stats.at[mine],
            dst_ref=stats.at[slot],
            send_sem=f_send.at[d],
            recv_sem=f_recv.at[slot],
            device_id={"fsdp": lax.rem(mine + d, fs)},
            device_id_type=MESH,
        )

    for d in range(1, fs):
        share(d, mine).start()
    for d in range(1, fs):
        share(d, lax.rem(mine + d, fs)).wait_recv()
    both = stats[0]
    for f in range(1, fs):
        both = both + stats[f]
    inv = lax.rsqrt(both[:, 0:1] / HD + EPS)
    mean = both[:, HEAD_DIM - 1 : HEAD_DIM] * inv / HD
    sq[...] = jnp.broadcast_to(inv, sq.shape)
    cr[...] = jnp.broadcast_to(mean, cr.shape)

    def grad_state(head):
        cols = cols_of(head)
        up = cot[:, cols].astype(F32)
        normed = att[:, cols] * sq[...]
        gp[i, :, cols] = jnp.sum(up * normed, axis=0, keepdims=True)
        d_h = ((up * gain_ref[:, cols] - normed * cr[...]) * sq[...]).astype(BF16)
        do[:, cols] = d_h
        return dot_atb(q[:, cols], d_h)

    make_states(scans[1], grad_state)

    def gain_near(d, slot):
        return pltpu.make_async_remote_copy(
            src_ref=gp.at[i],
            dst_ref=gp.at[slot],
            send_sem=g_send.at[d],
            recv_sem=g_recv.at[slot],
            device_id={"seq": z * g + lax.rem(i + d, g)},
            device_id_type=MESH,
        )

    def gain_far(d, slot):
        return pltpu.make_async_remote_copy(
            src_ref=gz.at[z],
            dst_ref=gz.at[slot],
            send_sem=h_send.at[d],
            recv_sem=h_recv.at[slot],
            device_id={"seq": lax.rem(z + d, m) * g + i},
            device_id_type=MESH,
        )

    for d in range(1, g):
        gain_near(d, i).start()

    def backward(head):
        cols = cols_of(head)
        qh, kh, vh, dh = q[:, cols], k[:, cols], v[:, cols], do[:, cols]
        q1, k0, v0, d1 = q[low, cols], k[top, cols], v[top, cols], do[low, cols]
        from_prefix = dot_abt(dh, state_at(scans[0], head))
        s0 = lower(dot_abt(do[top, cols], v0), 0)
        s1 = lower(dot_abt(d1, vh), half)
        qg[top, cols] = (dot_ab(s0, k0) + from_prefix[:half]).astype(BF16)
        qg[low, cols] = (dot_ab(s1, kh) + from_prefix[half:]).astype(BF16)
        t0 = upper(dot_abt(v0, dh))
        t1 = upper(dot_abt(v[low, cols], d1))
        kg_l[top, cols] = dot_ab(t0, qh)
        kg_l[low, cols] = dot_ab(t1, q1)
        vg_l[top, cols] = dot_ab(w_top[head], dh)
        vg_l[low, cols] = dot_ab(w_low[head], d1)

    beside(scans[1], backward, 1, 2)

    for d in range(1, g):
        gain_near(d, lax.rem(i + d, g)).wait_recv()
    near = gp[0]
    for p in range(1, g):
        near = near + gp[p]
    gz[z] = near
    for d in range(1, m):
        gain_far(d, z).start()

    def last(head):
        cols = cols_of(head)
        suffix = state_at(scans[1], head)
        kg[:, cols] = (kg_l[:, cols] + dot_abt(v[:, cols], suffix)).astype(BF16)
        vg[:, cols] = (vg_l[:, cols] + dot_ab(k[:, cols], suffix)).astype(BF16)

    arrivals(scans[1], last)

    for d in range(1, m):
        gain_far(d, lax.rem(z + d, m)).wait_recv()
    total = gz[0]
    for p in range(1, m):
        total = total + gz[p]
    gg_ref[...] = total * (1.0 / math.sqrt(rows * n))

    for scan in scans:
        scan.drain()
    for d in range(1, fs):
        share(d, mine).wait_send()
    for d in range(1, g):
        gain_near(d, i).wait_send()
    for d in range(1, m):
        gain_far(d, z).wait_send()


def store(qg, kg, vg, gg, qg_hbm, kg_hbm, vg_hbm, gg_hbm, sem):
    copies = [
        pltpu.make_async_copy(src, dst, sem.at[at])
        for at, (src, dst) in enumerate(((qg, qg_hbm), (kg, kg_hbm), (vg, vg_hbm), (gg, gg_hbm)))
    ]
    for copy in copies:
        copy.start()
    for copy in copies:
        copy.wait()


def solution(mesh):
    n, fs = mesh.shape["seq"], mesh.shape["fsdp"]
    g = group_size(n)
    m = n // g

    def shards(query, key, value, cotangent, gain):
        rows, width = query.shape
        heads = width // HEAD_DIM
        chunks = max(heads // g, 1)
        state = heads * HEAD_DIM
        piece = state // g
        levels = max(m.bit_length() - 1, 1)
        any_space = pl.BlockSpec(memory_space=pl.ANY)
        vmem = pl.BlockSpec(memory_space=pltpu.VMEM)
        dma = pltpu.SemaphoreType.DMA
        big, small = jax.ShapeDtypeStruct((rows, width), BF16), jax.ShapeDtypeStruct((1, width), F32)
        held = pltpu.VMEM((rows, width), BF16)
        products = 6 * rows * rows + 6 * rows * HEAD_DIM
        results = pl.pallas_call(
            functools.partial(kernel, n, g, fs, chunks),
            out_shape=(held, held, held, pltpu.VMEM((1, width), F32)),
            in_specs=[any_space] * 4 + [vmem],
            out_specs=(vmem, vmem, vmem, vmem),
            scratch_shapes=[pltpu.VMEM((rows, width), BF16)] * 5
            + [pltpu.VMEM((rows, width), F32)] * 3
            + [
                pltpu.VMEM((heads, rows // 2, rows), BF16),
                pltpu.VMEM((heads, rows // 2, rows // 2), BF16),
                pltpu.VMEM((2, state, HEAD_DIM), F32),
                pltpu.VMEM((2, g, piece, HEAD_DIM), F32),
                pltpu.VMEM((2, levels, piece, HEAD_DIM), F32),
                pltpu.VMEM((2, levels, piece, HEAD_DIM), F32),
                pltpu.VMEM((2, piece, HEAD_DIM), F32),
                pltpu.VMEM((2, g, piece, HEAD_DIM), F32),
                pltpu.VMEM((2, state, HEAD_DIM), F32),
                pltpu.VMEM((rows, HEAD_DIM), F32),
                pltpu.VMEM((rows, HEAD_DIM), F32),
                pltpu.VMEM((fs, rows, HEAD_DIM), F32),
                pltpu.VMEM((g, 1, width), F32),
                pltpu.VMEM((m, 1, width), F32),
                dma((4,)),
                dma((2, g, chunks)),
                dma((2, g, chunks)),
                dma((2, levels, max(m // 2, 1), chunks)),
                dma((2, levels, chunks)),
                dma((2, g, chunks)),
                dma((2, g, chunks)),
                dma((fs,)),
                dma((fs,)),
                dma((g,)),
                dma((g,)),
                dma((m,)),
                dma((m,)),
            ],
            compiler_params=pltpu.CompilerParams(
                collective_id=0, has_side_effects=True, vmem_limit_bytes=50 * 2**20
            ),
            cost_estimate=pl.CostEstimate(
                flops=2 * products * width, bytes_accessed=14 * rows * width, transcendentals=rows
            ),
        )(query, key, value, cotangent, gain.reshape(1, width))
        grads = pl.pallas_call(
            store,
            out_shape=(big, big, big, small),
            in_specs=[any_space] * 4,
            out_specs=(any_space,) * 4,
            scratch_shapes=[dma((4,))],
            compiler_params=pltpu.CompilerParams(vmem_limit_bytes=2**20),
        )(*results)
        return (*grads[:3], grads[3].reshape(width))

    in_specs = (P("seq", "fsdp"), P("seq", "fsdp"), P("seq", "fsdp"), P("seq", "fsdp"), P("fsdp"))
    out_specs = (P("seq", "fsdp"), P("seq", "fsdp"), P("seq", "fsdp"), P("fsdp"))
    return jax.shard_map(shards, mesh=mesh, in_specs=in_specs, out_specs=out_specs, check_vma=False)
```
